32 devices in a mesh: files: 2 (over y), ctx: 4 (over z), chan: 4 (over x, core).
Axes of the slice: x: 2, y: 2, z: 4, core: 2. Of those that a mesh axis runs over, the one named last changes fastest.
Arguments:
- activations: bfloat16 [4096, 4096], P(('files', 'ctx'), 'chan'), parts along dimension 0, may hold values from -6 to 6
- proj_weight: bfloat16 [3, 256, 4096], P(None, 'chan'), may hold values from -0.09375 to 0.09375
- long_filter: float32 [256, 2048], P('chan', 'ctx'), may hold values from -6 to 6
- skip_gain: float32 [256], P('chan'), may hold values from -1 to 1
- out_grad: bfloat16 [256, 4096], P('chan', ('files', 'ctx')), parts along dimension 1, may hold values from -6 to 6
Outputs:
- grad_input: bfloat16 [4096, 4096], P(('files', 'ctx'), 'chan'), parts along dimension 0
- grad_weight: float32 [6, 256, 4096], P('files', 'chan'), parts along dimension 0
- grad_filter: float32 [256, 4096], P('chan', ('files', 'ctx')), parts along dimension 1
The draws below stay inside these ranges and needn't reach their ends.
There are 2 independent parts, one for each index of `files`. The reference program is written for one: setup_inputs(seed, part) draws one part's arguments, and reference() takes and returns one part's arrays. A program takes and returns all parts, laid end to end along the dimension named above; an argument that names none is the same for every part. Nothing has to cross between parts.
All inputs are finite; a program needn't handle non-finite values.
Results may differ from the reference program's by a relative error of at most 0.0095.
Values may be sent and summed in bfloat16 or wider, within the bound.
No kernel may reach another device: no remote copies, remote signals or barrier semaphores. Data moves between devices by JAX's collectives and lax.ppermute only.
A program may use at most 64 MiB of HBM per device.

```python
import jax
import jax.numpy as jnp

D = 4096
C = 256
TOKENS = 2048


def levels(own_key, shape, cuts, smallest, largest):
    loudness = 1.0
    for position, shards_of in cuts:
        steps = jax.random.uniform(jax.random.fold_in(jax.random.fold_in(own_key, 6), position), (shards_of,), jnp.float32, smallest / len(cuts), largest / len(cuts))
        loudness = loudness * jnp.repeat(jnp.exp(steps), shape[position] // shards_of).reshape((-1,) + (1,) * (len(shape) - 1 - position))
    return loudness


def bell_draw(key, extent, scale, limit, cuts=(), dtype=jnp.bfloat16):
    drawn = jax.random.normal(key, extent, jnp.float32) * scale
    if len(cuts) > 0:
        drawn = levels(key, extent, cuts, -0.22, 0.18) * drawn
    return jnp.clip(drawn, min=-limit, max=limit).astype(dtype)


def setup_inputs(seed: int = 0, part: int = 0) -> dict:
    splits = jax.random.split(jax.random.key(seed), 6)
    part_keys = jax.random.split(jax.random.fold_in(splits[5], part), 6)
    activations = bell_draw(part_keys[0], (TOKENS, D), 1.0, 6.0, ((0, 4), (1, 4)))
    proj_weight = bell_draw(splits[1], (3, C, D), D ** -0.5, 0.09375, ((1, 4),))
    long_filter = bell_draw(splits[2], (C, TOKENS), 1.0, 6.0, ((0, 4), (1, 4)), jnp.float32)
    skip_gain = jnp.clip(jax.random.uniform(splits[3], (C,), jnp.float32, -1.0, 1.0) * levels(splits[3], (C,), ((0, 4),), -0.4, 0.0), -1.0, 1.0)
    out_grad = bell_draw(part_keys[4], (C, TOKENS), 1.0, 6.0, ((0, 4), (1, 4)))
    return {"activations": activations, "proj_weight": proj_weight, "long_filter": long_filter, "skip_gain": skip_gain, "out_grad": out_grad}


def reference(activations, proj_weight, long_filter, skip_gain, out_grad):
    factor = TOKENS ** -0.5
    projected = jnp.einsum('kcd,td->kct', proj_weight.astype(jnp.float32), activations.astype(jnp.float32)).astype(jnp.bfloat16)
    left_in = projected[0].astype(jnp.float32)
    right_in = projected[1].astype(jnp.float32)
    value_in = projected[2].astype(jnp.float32)
    gated = left_in * value_in
    filter_vals = long_filter * factor
    grad_conv = out_grad.astype(jnp.float32) * right_in
    padded_len = 2 * TOKENS
    spec_gated = jnp.fft.fft(gated, n=padded_len, axis=-1)
    spec_filter = jnp.fft.fft(filter_vals, n=padded_len, axis=-1)
    spec_grad = jnp.fft.fft(grad_conv, n=padded_len, axis=-1)
    conv_part = jnp.real(jnp.fft.ifft(spec_filter * spec_gated, axis=-1))[:, :TOKENS]
    conv_out = conv_part + skip_gain[:, None] * gated
    corr_part = jnp.real(jnp.fft.ifft(jnp.conj(spec_filter) * spec_grad, axis=-1))[:, :TOKENS]
    grad_gated = corr_part + skip_gain[:, None] * grad_conv
    grad_filter = factor * jnp.real(jnp.fft.ifft(jnp.conj(spec_gated) * spec_grad, axis=-1))[:, :TOKENS]
    grad_proj = jnp.stack([grad_gated * value_in, out_grad.astype(jnp.float32) * conv_out, grad_gated * left_in]).astype(jnp.bfloat16)
    grad_input = jnp.einsum('kct,kcd->td', grad_proj.astype(jnp.float32), proj_weight.astype(jnp.float32)).astype(jnp.bfloat16)
    grad_weight = factor * jnp.einsum('td,kct->kcd', activations.astype(jnp.float32), grad_proj.astype(jnp.float32))
    return grad_input, grad_weight, grad_filter
```

```python
import functools
import math

import jax
import jax.numpy as jnp
import numpy as np
from jax import lax
from jax.experimental import pallas as pl
from jax.experimental.pallas import tpu as pltpu
from jax.sharding import PartitionSpec as P

LANES = 128
BF16 = jnp.bfloat16
F32 = jnp.float32


def split_table(table):
    high = np.asarray(table, np.float32).astype(BF16)
    low = (np.asarray(table, np.float64) - high.astype(np.float64)).astype(BF16)
    return np.stack([high, low])


def fourier_tables(tokens, group):
    period = 2 * tokens
    rows = period // LANES
    used = rows // 2
    freqs = rows // 2 + 1
    part = -(-freqs * group // 8) * 8
    k1 = np.arange(freqs)
    n1 = np.arange(used)
    angle = 2.0 * math.pi * (np.outer(k1, n1) % rows) / rows
    eye = np.eye(group)
    forward = np.zeros((2 * part, used * group))
    forward[: freqs * group] = np.kron(np.cos(angle), eye)
    forward[part : part + freqs * group] = np.kron(-np.sin(angle), eye)
    weight = np.where((k1 == 0) | (k1 == rows // 2), 1.0, 2.0)[None, :] / period
    inverse = np.zeros((used * group, 2 * part))
    inverse[:, : freqs * group] = np.kron(np.cos(angle.T) * weight, eye)
    inverse[:, part : part + freqs * group] = np.kron(-np.sin(angle.T) * weight, eye)
    n2 = np.arange(LANES)
    turn = 2.0 * math.pi * np.outer(k1, n2) / period
    twiddle = np.zeros((2, part, LANES), np.float32)
    twiddle[0, : freqs * group] = np.repeat(np.cos(turn), group, axis=0)
    twiddle[1, : freqs * group] = np.repeat(np.sin(turn), group, axis=0)
    inner = 2.0 * math.pi * (np.outer(n2, n2) % LANES) / LANES
    cos, sin = np.cos(inner), np.sin(inner)
    second = np.block([[cos, -sin], [sin, cos]])
    second_back = np.block([[cos, sin], [-sin, cos]])
    return (
        split_table(forward),
        split_table(second),
        split_table(second_back),
        split_table(inverse),
        twiddle,
    )


def halves(values):
    high = values.astype(BF16)
    return high, (values - high.astype(F32)).astype(BF16)


def mm(left, right):
    return jnp.dot(left, right, preferred_element_type=F32)


def table_left(table, values):
    high, low = halves(values)
    return mm(table[0], high) + (mm(table[0], low) + mm(table[1], high))


def table_right(values, table):
    high, low = halves(values)
    return mm(high, table[0]) + (mm(low, table[0]) + mm(high, table[1]))


def conv_kernel(blocks, chans, group, factor, *refs):
    signal_refs = refs[:blocks]
    upstream_refs = refs[blocks : 2 * blocks]
    filter_refs = refs[2 * blocks : 3 * blocks]
    gain_ref, fwd_ref, second_ref, back_ref, inv_ref, twiddle_ref = refs[3 * blocks : 3 * blocks + 6]
    refs = refs[3 * blocks + 6 :]
    grad_refs = refs[:blocks]
    grad_filter_refs = refs[blocks : 2 * blocks]
    series, results = refs[2 * blocks :]
    place = lax.axis_index("ctx")
    length = series.shape[-1]
    cuts = length // LANES
    for m in range(blocks):
        where = place ^ m
        values = signal_refs[m][...].astype(F32)
        upstream = upstream_refs[m][...].astype(F32)
        series[0, where] = filter_refs[m][...] * factor
        series[1, where] = values[:chans] * values[2 * chans :]
        series[2, where] = upstream * values[chans : 2 * chans]
    part = twiddle_ref.shape[1]
    cos, sin = twiddle_ref[0], twiddle_ref[1]
    for start in range(0, chans, group):
        picked = []
        for q in range(3):
            tiles = []
            for z in range(blocks):
                loaded = series[q, z]
                loaded = loaded[start : start + group]
                for n in range(cuts):
                    tiles.append(loaded[:, n * LANES : (n + 1) * LANES])
            picked.append(jnp.concatenate(tiles, axis=0))
        first = table_left(fwd_ref, jnp.concatenate(picked, axis=1))
        turned = []
        for q in range(3):
            re = first[:part, q * LANES : (q + 1) * LANES]
            im = first[part:, q * LANES : (q + 1) * LANES]
            turned.append(jnp.concatenate([re * cos + im * sin, im * cos - re * sin], axis=1))
        spectra = table_right(jnp.concatenate(turned, axis=0), second_ref)
        parts = [
            (spectra[q * part : (q + 1) * part, :LANES], spectra[q * part : (q + 1) * part, LANES:])
            for q in range(3)
        ]
        (fr, fi), (gr, gi), (ur, ui) = parts
        products = jnp.concatenate(
            [
                jnp.concatenate([fr * gr - fi * gi, fr * gi + fi * gr], axis=1),
                jnp.concatenate([fr * ur + fi * ui, fr * ui - fi * ur], axis=1),
                jnp.concatenate([gr * ur + gi * ui, gr * ui - gi * ur], axis=1),
            ],
            axis=0,
        )
        back = table_right(products, back_ref)
        turned = []
        for q in range(3):
            re = back[q * part : (q + 1) * part, :LANES]
            im = back[q * part : (q + 1) * part, LANES:]
            turned.append(jnp.concatenate([re * cos - im * sin, im * cos + re * sin], axis=0))
        final = table_left(inv_ref, jnp.concatenate(turned, axis=1))
        for q in range(3):
            for z in range(blocks):
                tiles = [
                    final[(z * cuts + n) * group : (z * cuts + n + 1) * group, q * LANES : (q + 1) * LANES]
                    for n in range(cuts)
                ]
                results[q, z, start : start + group, :] = jnp.concatenate(tiles, axis=1)
    gain = gain_ref[...]
    for m in range(blocks):
        where = place ^ m
        values = signal_refs[m][...].astype(F32)
        upstream = upstream_refs[m][...].astype(F32)
        conv_out = results[0, where] + gain * series[1, where]
        grad_gated = results[1, where] + gain * series[2, where]
        grad_refs[m][...] = jnp.concatenate(
            [grad_gated * values[2 * chans :], upstream * conv_out, grad_gated * values[:chans]], axis=0
        ).astype(BF16)
        grad_filter_refs[m][...] = factor * results[2, where]


def convolve(signals, upstream, filters, gain):
    blocks = len(signals)
    chans, length = upstream[0].shape
    tokens = blocks * length
    group = max(1, min(chans, 8, LANES * LANES // tokens))
    tables = fourier_tables(tokens, group)
    vmem = pl.BlockSpec(memory_space=pltpu.VMEM)
    count = 3 * blocks + 6
    part = tables[4].shape[1]
    flops = 2 * 3 * (chans // group) * 3 * (4 * part * group * (tokens // LANES) * LANES + 2 * part * 256 * 256)
    outs = pl.pallas_call(
        functools.partial(conv_kernel, blocks, chans, group, tokens ** (-0.5)),
        out_shape=[jax.ShapeDtypeStruct((3 * chans, length), BF16)] * blocks
        + [jax.ShapeDtypeStruct((chans, length), F32)] * blocks,
        in_specs=[vmem] * count,
        out_specs=[vmem] * (2 * blocks),
        scratch_shapes=[pltpu.VMEM((3, blocks, chans, length), F32)] * 2,
        compiler_params=pltpu.CompilerParams(vmem_limit_bytes=40 * 2**20),
        cost_estimate=pl.CostEstimate(flops=flops, bytes_accessed=4 * 2**20, transcendentals=0),
        name="conv",
    )(*signals, *upstream, *filters, gain, *[jnp.asarray(t) for t in tables])
    return outs[:blocks], outs[blocks:]


def swap(values, axis, mask):
    if mask == 0:
        return values
    size = lax.axis_size(axis)
    return lax.ppermute(values, axis, [(i, i ^ mask) for i in range(size)])


def after(values, *others):
    return lax.optimization_barrier((values, *others))[0]


def sum_over_ctx(local, place):
    if lax.axis_size("ctx") != 4:
        return [lax.psum(x.astype(BF16), "ctx").astype(F32) for x in local]
    middle = (place == 1) | (place == 2)
    totals = []
    for x in local:
        from_end = lax.ppermute(x.astype(BF16), "ctx", [(0, 1), (3, 2)])
        pair = x + from_end.astype(F32)
        from_pair = lax.ppermute(pair.astype(BF16), "ctx", [(1, 2), (2, 1)])
        total = pair + from_pair.astype(F32)
        given = lax.ppermute(total.astype(BF16), "ctx", [(1, 0), (2, 3)])
        totals.append(jnp.where(middle, total, given.astype(F32)))
    return totals


def per_device(activations, proj_weight, long_filter, skip_gain, out_grad):
    blocks = lax.axis_size("ctx")
    slabs = lax.axis_size("chan")
    place = lax.axis_index("ctx")
    mine = lax.axis_index("chan")
    length, width = activations.shape
    kinds, own, depth = proj_weight.shape
    share = own // blocks
    factor = (length * blocks) ** (-0.5)
    rows = kinds * own

    upstream = [swap(lax.dynamic_slice_in_dim(out_grad, (place ^ m) * share, share, 0), "ctx", m) for m in range(blocks)]
    filters = [swap(lax.dynamic_slice_in_dim(long_filter, (place ^ m) * share, share, 0), "ctx", m) for m in range(blocks)]
    gain = lax.dynamic_slice_in_dim(skip_gain, place * share, share, 0)[:, None]

    if slabs == 4:
        far = swap(activations, "chan", 2)
        features = [activations, swap(activations, "chan", 1), far, swap(far, "chan", 1)]
    else:
        features = [swap(activations, "chan", m) for m in range(slabs)]

    def columns(array, m):
        return lax.dynamic_slice_in_dim(array, (mine ^ m) * width, width, array.ndim - 1)

    weight_rows = proj_weight.reshape(rows, depth)
    projected = 0.0
    for m in range(slabs):
        projected = projected + lax.dot_general(
            columns(weight_rows, m), features[m], (((1,), (1,)), ((), ())), preferred_element_type=F32
        )
    projected = projected.astype(BF16).reshape(kinds, own, length)

    held = after(proj_weight, features[slabs // 2])
    weight_cols = [swap(columns(held, m), "chan", m).reshape(rows, width) for m in range(slabs)]

    signals = [
        swap(
            lax.dynamic_slice_in_dim(projected, (place ^ m) * share, share, 1).reshape(kinds * share, length),
            "ctx",
            m,
        )
        for m in range(blocks)
    ]
    grads, grad_filters = convolve(signals, upstream, filters, gain)

    def collect(pieces, dtype, kinds):
        found = jnp.zeros((kinds, own, length), dtype)
        for m in range(blocks):
            piece = swap(pieces[m], "ctx", m).reshape(kinds, share, length)
            found = lax.dynamic_update_slice_in_dim(found, piece, (place ^ m) * share, 1)
        return found.reshape(kinds * own, length)

    grad_proj = collect(grads, BF16, kinds)
    grad_filter = collect(grad_filters, F32, 1)

    local = [mm(grad_proj, features[m]) for m in range(slabs)]
    totals = sum_over_ctx(local, place)
    grad_weight = jnp.zeros((rows, depth), F32)
    for m in range(slabs):
        grad_weight = lax.dynamic_update_slice_in_dim(grad_weight, totals[m] * factor, (mine ^ m) * width, 1)

    if slabs == 4:
        far = swap(grad_proj, "chan", 2)
        gathered = [grad_proj, swap(grad_proj, "chan", 1), far, swap(far, "chan", 1)]
    else:
        gathered = [swap(grad_proj, "chan", m) for m in range(slabs)]
    grad_rows = 0.0
    for m in range(slabs):
        grad_rows = grad_rows + lax.dot_general(
            gathered[m], weight_cols[m], (((0,), (0,)), ((), ())), preferred_element_type=F32
        )
    return (
        grad_rows.astype(BF16),
        grad_weight.reshape(kinds, own, depth),
        grad_filter,
    )


def solution(mesh):
    placed = (
        P(("files", "ctx"), "chan"),
        P(None, "chan", None),
        P("chan", "ctx"),
        P("chan"),
        P("chan", ("files", "ctx")),
    )
    return jax.shard_map(
        per_device,
        mesh=mesh,
        in_specs=placed,
        out_specs=(
            P(("files", "ctx"), "chan"),
            P("files", "chan", None),
            P("chan", ("files", "ctx")),
        ),
        check_vma=False,
    )
```

```python
import functools
import math

import jax
import jax.numpy as jnp
import numpy as np
from jax import lax
from jax.experimental import pallas as pl
from jax.experimental.pallas import tpu as pltpu
from jax.sharding import PartitionSpec as P

LANES = 128
BF16 = jnp.bfloat16
F32 = jnp.float32
VMEM = pl.BlockSpec(memory_space=pltpu.VMEM)
ANY = pl.BlockSpec(memory_space=pl.ANY)
HBM = pl.BlockSpec(memory_space=pltpu.HBM)


def split_table(table):
    high = np.asarray(table, np.float32).astype(BF16)
    low = (np.asarray(table, np.float64) - high.astype(np.float64)).astype(BF16)
    return np.stack([high, low])


def fourier_tables(tokens, group):
    period = 2 * tokens
    rows = period // LANES
    used = rows // 2
    freqs = rows // 2 + 1
    part = -(-freqs * group // 8) * 8
    k1 = np.arange(freqs)
    n1 = np.arange(used)
    angle = 2.0 * math.pi * (np.outer(k1, n1) % rows) / rows
    eye = np.eye(group)
    forward = np.zeros((2 * part, used * group))
    forward[: freqs * group] = np.kron(np.cos(angle), eye)
    forward[part : part + freqs * group] = np.kron(-np.sin(angle), eye)
    weight = np.where((k1 == 0) | (k1 == rows // 2), 1.0, 2.0)[None, :] / period
    inverse = np.zeros((used * group, 2 * part))
    inverse[:, : freqs * group] = np.kron(np.cos(angle.T) * weight, eye)
    inverse[:, part : part + freqs * group] = np.kron(-np.sin(angle.T) * weight, eye)
    n2 = np.arange(LANES)
    turn = 2.0 * math.pi * np.outer(k1, n2) / period
    twiddle = np.zeros((2, part, LANES), np.float32)
    twiddle[0, : freqs * group] = np.repeat(np.cos(turn), group, axis=0)
    twiddle[1, : freqs * group] = np.repeat(np.sin(turn), group, axis=0)
    inner = 2.0 * math.pi * (np.outer(n2, n2) % LANES) / LANES
    cos, sin = np.cos(inner), np.sin(inner)
    second = np.block([[cos, -sin], [sin, cos]])
    second_back = np.block([[cos, sin], [-sin, cos]])
    return (
        split_table(forward),
        split_table(second),
        split_table(second_back),
        split_table(inverse),
        twiddle,
    )


def halves(values):
    high = values.astype(BF16)
    return high, (values - high.astype(F32)).astype(BF16)


def mm(left, right):
    return jnp.dot(left, right, preferred_element_type=F32)


def table_left(table, values):
    high, low = halves(values)
    return mm(table[0], high) + (mm(table[0], low) + mm(table[1], high))


def table_right(values, table):
    high, low = halves(values)
    return mm(high, table[0]) + (mm(low, table[0]) + mm(high, table[1]))


def conv_kernel(blocks, chans, group, factor, *refs):
    count = 2 * blocks + 5
    gain_ref, sources, refs = refs[0], refs[1 : 1 + count], refs[1 + count :]
    out_refs = refs[:blocks]
    series, results, inputs = refs[blocks : 3 + blocks]
    held = refs[3 + blocks : 3 + blocks + count]
    sems = refs[3 + blocks + count]
    copies = [pltpu.make_async_copy(sources[i], held[i], sems.at[i]) for i in range(count)]
    for copy in copies:
        copy.start()
    ready_refs, signal_refs = held[:blocks], held[blocks : 2 * blocks]
    fwd_ref, second_ref, back_ref, inv_ref, twiddle_ref = held[2 * blocks :]
    place = lax.axis_index("ctx")
    length = series.shape[-1]
    cuts = length // LANES
    for m in range(blocks):
        where = place ^ m
        copies[m].wait()
        copies[blocks + m].wait()
        values = signal_refs[m][...].astype(F32)
        upstream = ready_refs[m][:chans, :]
        inputs[0, where] = values[:chans]
        inputs[1, where] = values[2 * chans :]
        inputs[2, where] = upstream
        series[0, where] = ready_refs[m][chans:, :] * factor
        series[1, where] = values[:chans] * values[2 * chans :]
        series[2, where] = upstream * values[chans : 2 * chans]
    for copy in copies[2 * blocks :]:
        copy.wait()
    part = twiddle_ref.shape[1]
    cos, sin = twiddle_ref[0], twiddle_ref[1]
    for start in range(0, chans, group):
        picked = []
        for q in range(3):
            tiles = []
            for z in range(blocks):
                loaded = series[q, z]
                loaded = loaded[start : start + group]
                for n in range(cuts):
                    tiles.append(loaded[:, n * LANES : (n + 1) * LANES])
            picked.append(jnp.concatenate(tiles, axis=0))
        first = table_left(fwd_ref, jnp.concatenate(picked, axis=1))
        turned = []
        for q in range(3):
            re = first[:part, q * LANES : (q + 1) * LANES]
            im = first[part:, q * LANES : (q + 1) * LANES]
            turned.append(jnp.concatenate([re * cos + im * sin, im * cos - re * sin], axis=1))
        spectra = table_right(jnp.concatenate(turned, axis=0), second_ref)
        parts = [
            (spectra[q * part : (q + 1) * part, :LANES], spectra[q * part : (q + 1) * part, LANES:])
            for q in range(3)
        ]
        (fr, fi), (gr, gi), (ur, ui) = parts
        products = jnp.concatenate(
            [
                jnp.concatenate([fr * gr - fi * gi, fr * gi + fi * gr], axis=1),
                jnp.concatenate([fr * ur + fi * ui, fr * ui - fi * ur], axis=1),
                jnp.concatenate([gr * ur + gi * ui, gr * ui - gi * ur], axis=1),
            ],
            axis=0,
        )
        back = table_right(products, back_ref)
        turned = []
        for q in range(3):
            re = back[q * part : (q + 1) * part, :LANES]
            im = back[q * part : (q + 1) * part, LANES:]
            turned.append(jnp.concatenate([re * cos - im * sin, im * cos + re * sin], axis=0))
        final = table_left(inv_ref, jnp.concatenate(turned, axis=1))
        for q in range(3):
            for z in range(blocks):
                tiles = [
                    final[(z * cuts + n) * group : (z * cuts + n + 1) * group, q * LANES : (q + 1) * LANES]
                    for n in range(cuts)
                ]
                results[q, z, start : start + group, :] = jnp.concatenate(tiles, axis=1)
    gain = gain_ref[...]
    for z in range(blocks):
        conv_out = results[0, z] + gain * series[1, z]
        grad_gated = results[1, z] + gain * series[2, z]
        grads = jnp.concatenate(
            [grad_gated * inputs[1, z], inputs[2, z] * conv_out, grad_gated * inputs[0, z]], axis=0
        ).astype(BF16)
        for ref in out_refs:
            ref[:, z * length : (z + 1) * length] = grads
    for m in range(blocks):
        found = factor * results[2, place ^ m]
        half = length // 2
        rows = jnp.concatenate([found[:, :half], found[:, half:], jnp.zeros((chans, half), F32)], axis=0)
        out_refs[m][:, blocks * length :] = rows.astype(BF16)


def convolve(signals, ready, gain):
    blocks = len(ready)
    chans, length = ready[0].shape[0] // 2, ready[0].shape[1]
    tokens = blocks * length
    group = max(1, min(chans, 8, LANES * LANES // tokens))
    tables = fourier_tables(tokens, group)
    arrays = [*ready, *signals, *[jnp.asarray(table) for table in tables]]
    part = tables[4].shape[1]
    flops = 2 * 3 * (chans // group) * 3 * (4 * part * group * (tokens // LANES) * LANES + 2 * part * 256 * 256)
    return pl.pallas_call(
        functools.partial(conv_kernel, blocks, chans, group, tokens ** (-0.5)),
        out_shape=[jax.ShapeDtypeStruct((3 * chans, tokens + length // 2), BF16)] * blocks,
        in_specs=[VMEM] + [HBM] * len(arrays),
        out_specs=[VMEM] * blocks,
        scratch_shapes=[pltpu.VMEM((3, blocks, chans, length), F32)] * 3
        + [pltpu.VMEM(array.shape, array.dtype) for array in arrays]
        + [pltpu.SemaphoreType.DMA((len(arrays),))],
        compiler_params=pltpu.CompilerParams(vmem_limit_bytes=40 * 2**20),
        cost_estimate=pl.CostEstimate(flops=flops, bytes_accessed=4 * 2**20, transcendentals=0),
        name="conv",
    )(gain, *arrays)


def partial_rows(weight_ref, refs, masks):
    mine = lax.axis_index("chan")
    sums = 0.0
    for m, ref in zip(masks, refs):
        width = ref.shape[1]
        at = pl.multiple_of((mine ^ m) * width, width)
        sums = sums + lax.dot_general(
            ref[...], weight_ref[:, pl.ds(at, width)], (((1,), (1,)), ((), ())), preferred_element_type=F32
        )
    return sums


def start_kernel(masks, weight_ref, *refs):
    refs[-1][...] = partial_rows(weight_ref, refs[:-1], masks)


def more_kernel(masks, weight_ref, sum_ref, *refs):
    refs[-1][...] = sum_ref[...] + partial_rows(weight_ref, refs[:-1], masks)


def finish_kernel(masks, blocks, kinds, share, weight_ref, sum_ref, *refs):
    out_refs = refs[len(masks) : len(masks) + blocks]
    total = refs[-1]
    place = lax.axis_index("ctx")
    total[...] = (sum_ref[...] + partial_rows(weight_ref, refs[: len(masks)], masks)).T
    for m in range(blocks):
        first = (place ^ m) * share
        rows = [total[pl.ds(pl.multiple_of(k * share * blocks + first, share), share), :] for k in range(kinds)]
        out_refs[m][...] = jnp.concatenate(rows, axis=0).astype(BF16)


def project(weight_rows, features, groups, blocks, kinds):
    rows, depth = weight_rows.shape
    length = features[0].shape[0]
    share = rows // kinds // blocks
    sums = []
    for i, masks in enumerate(groups):
        last = i == len(groups) - 1
        if last:
            body = functools.partial(finish_kernel, masks, blocks, kinds, share)
            shape = [jax.ShapeDtypeStruct((kinds * share, length), BF16)] * blocks
        else:
            body = functools.partial(more_kernel if i else start_kernel, masks)
            shape = [jax.ShapeDtypeStruct((length, rows), F32)]
        picked = [features[m] for m in masks]
        flops = 2 * rows * length * depth * len(masks) // len(features)
        sums = pl.pallas_call(
            body,
            out_shape=shape,
            in_specs=[VMEM] * (1 + len(sums) + len(picked)),
            out_specs=[VMEM] * len(shape),
            scratch_shapes=[pltpu.VMEM((rows, length), F32)] if last else [],
            compiler_params=pltpu.CompilerParams(vmem_limit_bytes=40 * 2**20),
            cost_estimate=pl.CostEstimate(flops=flops, bytes_accessed=2**20, transcendentals=0),
            name="project",
        )(weight_rows, *sums, *picked)
    return sums


def product_kernel(kinds, share, blocks, slabs, *refs):
    grad_refs = refs[:blocks]
    sources = refs[blocks : blocks + slabs]
    first_ref, second_ref, own_ref, filter_ref = refs[blocks + slabs : blocks + slabs + 4]
    turned, sems = refs[blocks + slabs + 4 :]
    place = lax.axis_index("ctx")
    length = own_ref.shape[1]
    width = sources[0].shape[1]
    copies = [pltpu.make_async_copy(sources[i], turned.at[i], sems.at[i]) for i in range(slabs)]
    for copy in copies:
        copy.start()
    mine = pl.ds(pl.multiple_of(place * length, length), length)
    for m in range(blocks):
        for k in range(kinds):
            to = pl.multiple_of(k * share * blocks + (place ^ m) * share, share)
            own_ref[pl.ds(to, share), :] = grad_refs[m][k * share : (k + 1) * share, mine]
        to = pl.multiple_of((place ^ m) * share, share)
        end = grad_refs[m][:, blocks * length :].astype(F32)
        filter_ref[pl.ds(to, share), :] = jnp.concatenate([end[:share], end[share : 2 * share]], axis=1)
    left = []
    for b in range(blocks):
        columns = pl.ds(pl.multiple_of((place ^ b) * length, length), length)
        left.append(jnp.concatenate([ref[:, columns] for ref in grad_refs], axis=0))
    left = jnp.concatenate(left, axis=1)
    half = left.shape[0] // 2
    for i in range(slabs):
        copies[i].wait()
        value = mm(left, turned[i]).astype(BF16)
        first_ref[:, i * width : (i + 1) * width] = value[:half]
        second_ref[:, i * width : (i + 1) * width] = value[half:]


def weight_products(grads, turned, kinds, share):
    blocks, slabs = len(grads), len(turned)
    tokens, width = turned[0].shape
    rows = kinds * share
    half = jax.ShapeDtypeStruct((rows * blocks // 2, width * slabs), BF16)
    return pl.pallas_call(
        functools.partial(product_kernel, kinds, share, blocks, slabs),
        out_shape=[
            half,
            half,
            jax.ShapeDtypeStruct((rows * blocks, tokens // blocks), BF16),
            jax.ShapeDtypeStruct((share * blocks, tokens // blocks), F32),
        ],
        in_specs=[VMEM] * blocks + [ANY] * slabs,
        out_specs=[VMEM] * 4,
        scratch_shapes=[pltpu.VMEM((slabs, tokens, width), BF16), pltpu.SemaphoreType.DMA((slabs,))],
        compiler_params=pltpu.CompilerParams(vmem_limit_bytes=40 * 2**20),
        cost_estimate=pl.CostEstimate(
            flops=2 * rows * blocks * tokens * width * slabs, bytes_accessed=6 * 2**20, transcendentals=0
        ),
        name="products",
    )(*grads, *turned)


def input_kernel(count, *refs):
    sums = 0.0
    for grad_ref, weight_ref in zip(refs[:count], refs[count : 2 * count]):
        sums = sums + lax.dot_general(
            grad_ref[...], weight_ref[...], (((0,), (0,)), ((), ())), preferred_element_type=F32
        )
    refs[-1][...] = sums.astype(BF16)


def input_gradient(grads, weights):
    rows, length = grads[0].shape
    width = weights[0].shape[1]
    return pl.pallas_call(
        functools.partial(input_kernel, len(grads)),
        out_shape=jax.ShapeDtypeStruct((length, width), BF16),
        in_specs=[VMEM] * (2 * len(grads)),
        out_specs=VMEM,
        compiler_params=pltpu.CompilerParams(vmem_limit_bytes=40 * 2**20),
        cost_estimate=pl.CostEstimate(
            flops=2 * rows * len(grads) * length * width, bytes_accessed=4 * 2**20, transcendentals=0
        ),
        name="inputs",
    )(*grads, *weights)


def place_kernel(kinds, share, factor, *refs):
    out_ref = refs[-1]
    blocks = (len(refs) - 1) // 2
    place = lax.axis_index("ctx")
    slab = lax.axis_index("chan") ^ pl.program_id(0)
    width = out_ref.shape[1] // blocks
    source = pl.ds(pl.multiple_of(slab * width, width), width)
    for a in range(2):
        for r in range(blocks):
            sender = lax.rem(place + (r if a else blocks - r), blocks)
            columns = pl.ds(pl.multiple_of(sender * width, width), width)
            for b in range(2):
                for k in range(kinds):
                    row = (b * kinds + k) * share
                    value = refs[a * blocks + r][row : row + share, source].astype(F32) * factor
                    to = pl.multiple_of(k * share * blocks + (sender ^ (2 * a + b)) * share, share)
                    out_ref[pl.ds(to, share), columns] = value


def place_weights(pieces, kinds, share, slabs, factor):
    flat = [piece for group in pieces for piece in group]
    depth = flat[0].shape[1]
    rows = kinds * share * len(pieces[0])
    return pl.pallas_call(
        functools.partial(place_kernel, kinds, share, factor),
        out_shape=jax.ShapeDtypeStruct((rows, depth * slabs), F32),
        grid=(slabs,),
        in_specs=[pl.BlockSpec(flat[0].shape, lambda i: (0, 0))] * len(flat),
        out_specs=pl.BlockSpec((rows, depth), lambda i: (0, i)),
        compiler_params=pltpu.CompilerParams(vmem_limit_bytes=40 * 2**20),
        cost_estimate=pl.CostEstimate(flops=0, bytes_accessed=6 * 2**20, transcendentals=0),
        name="place",
    )(*flat)


def swap(values, axis, mask):
    if mask == 0:
        return values
    size = lax.axis_size(axis)
    return lax.ppermute(values, axis, [(i, i ^ mask) for i in range(size)])


def after(values, *others):
    return lax.optimization_barrier((values, *others))[0]


def gather_chan(values):
    slabs = lax.axis_size("chan")
    if slabs != 4:
        return [swap(values, "chan", m) for m in range(slabs)]
    far = swap(values, "chan", 2)
    return [values, swap(values, "chan", 1), far, swap(far, "chan", 1)]


def ring(values, step):
    size = lax.axis_size("ctx")
    found = [values]
    while len(found) < size:
        found.append(lax.ppermute(found[-1], "ctx", [(i, (i + step) % size) for i in range(size)]))
    return found


def general_tail(messages, features, place, mine, kinds, share, factor):
    blocks = lax.axis_size("ctx")
    length, width = features[0].shape
    rows = kinds * share * blocks
    grad_proj = jnp.zeros((kinds, share * blocks, length), BF16)
    grad_filter = jnp.zeros((share * blocks, length), F32)
    for m, message in enumerate(messages):
        piece = lax.dynamic_slice_in_dim(message, (place ^ m) * length, length, 1)
        piece = swap(piece, "ctx", m).reshape(kinds, share, length)
        grad_proj = lax.dynamic_update_slice_in_dim(grad_proj, piece, (place ^ m) * share, 1)
        end = swap(message[: 2 * share, blocks * length :], "ctx", m).astype(F32)
        end = jnp.concatenate([end[:share], end[share:]], axis=1)
        grad_filter = lax.dynamic_update_slice_in_dim(grad_filter, end, (place ^ m) * share, 0)
    grad_proj = grad_proj.reshape(rows, length)
    grad_weight = jnp.zeros((rows, width * len(features)), F32)
    for m, slab in enumerate(features):
        total = lax.psum(mm(grad_proj, slab).astype(BF16), "ctx").astype(F32) * factor
        grad_weight = lax.dynamic_update_slice_in_dim(grad_weight, total, (mine ^ m) * width, 1)
    return grad_proj, grad_weight, grad_filter


def per_device(activations, proj_weight, long_filter, skip_gain, out_grad):
    blocks = lax.axis_size("ctx")
    slabs = lax.axis_size("chan")
    place = lax.axis_index("ctx")
    mine = lax.axis_index("chan")
    length, width = activations.shape
    kinds, own, depth = proj_weight.shape
    share = own // blocks
    factor = (length * blocks) ** (-0.5)
    rows = kinds * own
    line = blocks == 4 and slabs == 4 and width % (blocks * LANES) == 0 and share % 16 == 0
    weight_rows = proj_weight.reshape(rows, depth)

    def share_of(array, m, axis=0, size=share):
        return lax.dynamic_slice_in_dim(array, (place ^ m) * size, size, axis)

    if line:
        features = [activations, swap(activations, "chan", 1), swap(activations, "chan", 2)]
        quarter = width // blocks
        turned = [swap(share_of(activations, m, 1, quarter), "ctx", m) for m in range(blocks)]
    else:
        features = [swap(activations, "chan", m) for m in range(slabs)]

    ready = jnp.stack([out_grad.astype(F32), long_filter], axis=1).reshape(blocks, share, 2, length)
    ready = jnp.swapaxes(ready, 1, 2).reshape(blocks * 2 * share, length)
    ready = [share_of(ready, m, 0, 2 * share) for m in range(blocks)]
    ready = after(ready, features[1])
    ready = [swap(piece, "ctx", m) for m, piece in enumerate(ready)]
    gain = share_of(skip_gain, 0)[:, None]

    groups = [[0, 1], [2], [3]] if line else [[0], list(range(1, slabs))]
    if line:
        features[2], turned, ready = lax.optimization_barrier((features[2], turned, ready))
        features.append(swap(features[2], "chan", 1))
        turned = jnp.concatenate(turned, axis=0)
        far = swap(turned, "chan", 2)
        turned = [turned, swap(turned, "chan", 1), far]

    pieces = project(weight_rows, features, groups, blocks, kinds)
    signals = [swap(piece, "ctx", m) for m, piece in enumerate(pieces)]
    messages = convolve(signals, ready, gain)
    if line:
        turned.append(swap(after(far, messages[0]), "chan", 1))

    weight_cols = [lax.dynamic_slice_in_dim(weight_rows, (mine ^ m) * width, width, 1) for m in range(slabs)]
    weight_cols = after(weight_cols, turned[2] if line else signals[-1])
    weight_cols = [swap(cols, "chan", m) for m, cols in enumerate(weight_cols)]

    if line:
        messages = [swap(message, "ctx", m) for m, message in enumerate(messages)]
        first, second, grad_proj, grad_filter = weight_products(messages, turned, kinds, share)
        pieces = [ring(first, 1), ring(second, -1)]
        grad_weight = place_weights(pieces, kinds, share, slabs, factor)
    else:
        grad_proj, grad_weight, grad_filter = general_tail(messages, features, place, mine, kinds, share, factor)

    return (
        input_gradient(gather_chan(grad_proj), weight_cols),
        grad_weight.reshape(kinds, own, depth),
        grad_filter,
    )


def solution(mesh):
    placed = (
        P(("files", "ctx"), "chan"),
        P(None, "chan", None),
        P("chan", "ctx"),
        P("chan"),
        P("chan", ("files", "ctx")),
    )
    return jax.shard_map(
        per_device,
        mesh=mesh,
        in_specs=placed,
        out_specs=(
            P(("files", "ctx"), "chan"),
            P("files", "chan", None),
            P("chan", ("files", "ctx")),
        ),
        check_vma=False,
    )
```

```python
import functools
import math

import jax
import jax.numpy as jnp
import numpy as np
from jax import lax
from jax.experimental import pallas as pl
from jax.experimental.pallas import tpu as pltpu
from jax.sharding import PartitionSpec as P

LANES = 128
BF16 = jnp.bfloat16
F32 = jnp.float32
VMEM = pl.BlockSpec(memory_space=pltpu.VMEM)
ANY = pl.BlockSpec(memory_space=pl.ANY)
VMEM_BYTES = 16 * 2**20


def split_table(table):
    high = np.asarray(table, np.float32).astype(BF16)
    low = (np.asarray(table, np.float64) - high.astype(np.float64)).astype(BF16)
    return np.stack([high, low])


def fourier_tables(tokens, group):
    period = 2 * tokens
    rows = period // LANES
    used = rows // 2
    freqs = rows // 2 + 1
    part = -(-freqs * group // 8) * 8
    k1 = np.arange(freqs)
    n1 = np.arange(used)
    angle = 2.0 * math.pi * (np.outer(k1, n1) % rows) / rows
    eye = np.eye(group)
    forward = np.zeros((2 * part, used * group))
    forward[: freqs * group] = np.kron(np.cos(angle), eye)
    forward[part : part + freqs * group] = np.kron(-np.sin(angle), eye)
    weight = np.where((k1 == 0) | (k1 == rows // 2), 1.0, 2.0)[None, :] / period
    inverse = np.zeros((used * group, 2 * part))
    inverse[:, : freqs * group] = np.kron(np.cos(angle.T) * weight, eye)
    inverse[:, part : part + freqs * group] = np.kron(-np.sin(angle.T) * weight, eye)
    n2 = np.arange(LANES)
    turn = 2.0 * math.pi * np.outer(k1, n2) / period
    twiddle = np.zeros((2, part, LANES), np.float32)
    twiddle[0, : freqs * group] = np.repeat(np.cos(turn), group, axis=0)
    twiddle[1, : freqs * group] = np.repeat(np.sin(turn), group, axis=0)
    inner = 2.0 * math.pi * (np.outer(n2, n2) % LANES) / LANES
    cos, sin = np.cos(inner), np.sin(inner)
    second = np.block([[cos, -sin], [sin, cos]])
    second_back = np.block([[cos, sin], [-sin, cos]])
    return (
        split_table(forward),
        split_table(second),
        split_table(second_back),
        split_table(inverse),
        twiddle,
    )


def halves(values):
    high = values.astype(BF16)
    return high, (values - high.astype(F32)).astype(BF16)


def mm(left, right):
    return jnp.dot(left, right, preferred_element_type=F32)


def table_left(table, values):
    high, low = halves(values)
    return mm(table[0], high) + (mm(table[0], low) + mm(table[1], high))


def table_right(values, table):
    high, low = halves(values)
    return mm(high, table[0]) + (mm(low, table[0]) + mm(high, table[1]))


def conv_kernel(blocks, chans, group, factor, *refs):
    count = blocks + 5
    gain_ref, sources, refs = refs[0], refs[1 : 1 + count], refs[1 + count :]
    out_refs = refs[:blocks]
    series, results, inputs = refs[blocks : 3 + blocks]
    held = refs[3 + blocks : 3 + blocks + count]
    sems = refs[3 + blocks + count]
    copies = [pltpu.make_async_copy(sources[i], held[i], sems.at[i]) for i in range(count)]
    for copy in copies:
        copy.start()
    signal_refs = held[:blocks]
    fwd_ref, second_ref, back_ref, inv_ref, twiddle_ref = held[blocks:]
    place = lax.axis_index("ctx")
    length = series.shape[-1]
    cuts = length // LANES
    for m in range(blocks):
        where = place ^ m
        copies[m].wait()
        values = signal_refs[m][...].astype(F32)
        upstream = values[3 * chans : 4 * chans]
        inputs[0, where] = values[:chans]
        inputs[1, where] = values[2 * chans : 3 * chans]
        inputs[2, where] = upstream
        series[0, where] = values[4 * chans :] * factor
        series[1, where] = values[:chans] * values[2 * chans : 3 * chans]
        series[2, where] = upstream * values[chans : 2 * chans]
    for copy in copies[blocks:]:
        copy.wait()
    part = twiddle_ref.shape[1]
    cos, sin = twiddle_ref[0], twiddle_ref[1]
    for start in range(0, chans, group):
        picked = []
        for q in range(3):
            tiles = []
            for z in range(blocks):
                loaded = series[q, z]
                loaded = loaded[start : start + group]
                for n in range(cuts):
                    tiles.append(loaded[:, n * LANES : (n + 1) * LANES])
            picked.append(jnp.concatenate(tiles, axis=0))
        first = table_left(fwd_ref, jnp.concatenate(picked, axis=1))
        turned = []
        for q in range(3):
            re = first[:part, q * LANES : (q + 1) * LANES]
            im = first[part:, q * LANES : (q + 1) * LANES]
            turned.append(jnp.concatenate([re * cos + im * sin, im * cos - re * sin], axis=1))
        spectra = table_right(jnp.concatenate(turned, axis=0), second_ref)
        parts = [
            (spectra[q * part : (q + 1) * part, :LANES], spectra[q * part : (q + 1) * part, LANES:])
            for q in range(3)
        ]
        (fr, fi), (gr, gi), (ur, ui) = parts
        products = jnp.concatenate(
            [
                jnp.concatenate([fr * gr - fi * gi, fr * gi + fi * gr], axis=1),
                jnp.concatenate([fr * ur + fi * ui, fr * ui - fi * ur], axis=1),
                jnp.concatenate([gr * ur + gi * ui, gr * ui - gi * ur], axis=1),
            ],
            axis=0,
        )
        back = table_right(products, back_ref)
        turned = []
        for q in range(3):
            re = back[q * part : (q + 1) * part, :LANES]
            im = back[q * part : (q + 1) * part, LANES:]
            turned.append(jnp.concatenate([re * cos - im * sin, im * cos + re * sin], axis=0))
        final = table_left(inv_ref, jnp.concatenate(turned, axis=1))
        for q in range(3):
            for z in range(blocks):
                tiles = [
                    final[(z * cuts + n) * group : (z * cuts + n + 1) * group, q * LANES : (q + 1) * LANES]
                    for n in range(cuts)
                ]
                results[q, z, start : start + group, :] = jnp.concatenate(tiles, axis=1)
    gain = gain_ref[...]
    for z in range(blocks):
        conv_out = results[0, z] + gain * series[1, z]
        grad_gated = results[1, z] + gain * series[2, z]
        grads = jnp.concatenate(
            [grad_gated * inputs[1, z], inputs[2, z] * conv_out, grad_gated * inputs[0, z]], axis=0
        ).astype(BF16)
        for ref in out_refs:
            ref[:, z * length : (z + 1) * length] = grads
    found = [(factor * results[2, place ^ m]).astype(BF16).astype(F32) for m in range(blocks)]
    cut = 3 * length // 4
    rest = jnp.zeros((chans, length - cut), F32)
    for m in range(blocks):
        pair = found[m], found[min(m ^ 1, blocks - 1)]
        last = jnp.concatenate([pair[0][:, cut:], pair[1][:, cut:], rest], axis=1)
        rows = jnp.concatenate([pair[0][:, :cut], pair[1][:, :cut], last], axis=0)
        out_refs[m][:, blocks * length :] = rows.astype(BF16)


def convolve(signals, gain):
    blocks = len(signals)
    chans, length = signals[0].shape[0] // 5, signals[0].shape[1]
    tokens = blocks * length
    group = max(1, min(chans, 8, LANES * LANES // tokens))
    tables = fourier_tables(tokens, group)
    arrays = [*signals, *[jnp.asarray(table) for table in tables]]
    part = tables[4].shape[1]
    flops = 2 * 3 * (chans // group) * 3 * (4 * part * group * (tokens // LANES) * LANES + 2 * part * 256 * 256)
    return pl.pallas_call(
        functools.partial(conv_kernel, blocks, chans, group, tokens ** (-0.5)),
        out_shape=[jax.ShapeDtypeStruct((3 * chans, tokens + 3 * length // 4), BF16)] * blocks,
        in_specs=[VMEM] + [ANY] * len(arrays),
        out_specs=[VMEM] * blocks,
        scratch_shapes=[pltpu.VMEM((3, blocks, chans, length), F32)] * 3
        + [pltpu.VMEM(array.shape, array.dtype) for array in arrays]
        + [pltpu.SemaphoreType.DMA((len(arrays),))],
        compiler_params=pltpu.CompilerParams(vmem_limit_bytes=60 * 2**20),
        cost_estimate=pl.CostEstimate(flops=flops, bytes_accessed=4 * 2**20, transcendentals=0),
        name="conv",
    )(gain, *arrays)


def partial_rows(weight_ref, refs, masks):
    mine = lax.axis_index("chan")
    sums = 0.0
    for m, ref in zip(masks, refs):
        width = ref.shape[1]
        at = pl.multiple_of((mine ^ m) * width, width)
        sums = sums + lax.dot_general(
            ref[...], weight_ref[:, pl.ds(at, width)], (((1,), (1,)), ((), ())), preferred_element_type=F32
        )
    return sums


def start_kernel(masks, weight_ref, *refs):
    refs[-1][...] = partial_rows(weight_ref, refs[:-1], masks)


def more_kernel(masks, weight_ref, sum_ref, *refs):
    refs[-1][...] = sum_ref[...] + partial_rows(weight_ref, refs[:-1], masks)


def finish_kernel(masks, blocks, kinds, share, given_ref, filter_ref, weight_ref, sum_ref, *refs):
    out_refs = refs[len(masks) : len(masks) + blocks]
    total = refs[-1]
    place = lax.axis_index("ctx")
    total[...] = (sum_ref[...] + partial_rows(weight_ref, refs[: len(masks)], masks)).T
    for m in range(blocks):
        first = (place ^ m) * share
        rows = [total[pl.ds(pl.multiple_of(k * share * blocks + first, share), share), :] for k in range(kinds)]
        for ref in (given_ref, filter_ref):
            rows.append(ref[pl.ds(pl.multiple_of(first, share), share), :])
        out_refs[m][...] = jnp.concatenate(rows, axis=0).astype(BF16)


def project(weight_rows, sums, features, masks, out=None):
    rows, depth = weight_rows.shape
    length, width = features[0].shape
    along = []
    if out is None:
        body = functools.partial(more_kernel if sums else start_kernel, masks)
        shape = [jax.ShapeDtypeStruct((length, rows), F32)]
    else:
        blocks, kinds, along = out
        share = rows // kinds // blocks
        body = functools.partial(finish_kernel, masks, blocks, kinds, share)
        shape = [jax.ShapeDtypeStruct(((kinds + 2) * share, length), BF16)] * blocks
    flops = 2 * rows * length * width * len(masks)
    return pl.pallas_call(
        body,
        out_shape=shape,
        in_specs=[VMEM] * (len(along) + 1 + len(sums) + len(features)),
        out_specs=[VMEM] * len(shape),
        scratch_shapes=[pltpu.VMEM((rows, length), F32)] if out else [],
        compiler_params=pltpu.CompilerParams(vmem_limit_bytes=VMEM_BYTES),
        cost_estimate=pl.CostEstimate(flops=flops, bytes_accessed=2**20, transcendentals=0),
        name="project",
    )(*along, weight_rows, *sums, *features)


def product_kernel(kinds, share, blocks, slabs, *refs):
    grad_refs, turned = refs[: blocks + 1], refs[blocks + 1 : blocks + 1 + slabs]
    left_ref, some_ref, own_ref, filter_ref = refs[blocks + 1 + slabs :]
    place = lax.axis_index("ctx")
    length = own_ref.shape[1]
    width = turned[0].shape[1]
    rows = kinds * share
    tokens = blocks * length
    mine = pl.ds(pl.multiple_of(place * length, length), length)
    middle = (place == 1) | (place == 2)
    for m in range(blocks):
        value = grad_refs[m][:, :tokens]
        if m == blocks - 1:
            value = value + grad_refs[blocks][:, :tokens]
        left_ref[m * rows : (m + 1) * rows, :] = value
        for k in range(kinds):
            to = pl.multiple_of(k * share * blocks + (place ^ m) * share, share)
            own_ref[pl.ds(to, share), :] = left_ref[m * rows + k * share : m * rows + (k + 1) * share, mine]
        end = grad_refs[m][:, tokens:].astype(F32)
        cut = end.shape[1]
        size = length - cut
        given = jnp.concatenate([end[:share], end[2 * share :, :size]], axis=1)
        if m == blocks - 1:
            end = grad_refs[blocks][:, tokens:].astype(F32)
            handed = jnp.concatenate([end[share : 2 * share], end[2 * share :, size : 2 * size]], axis=1)
            given = jnp.where(middle, given, handed)
        to = pl.multiple_of((place ^ m) * share, share)
        filter_ref[pl.ds(to, share), :] = given
    for i in range(slabs):
        some_ref[:, i * width : (i + 1) * width] = mm(left_ref[...], turned[i][...]).astype(BF16)


def last_kernel(left_ref, some_ref, turned_ref, first_ref, second_ref):
    half, known = first_ref.shape[0], some_ref.shape[1]
    value = mm(left_ref[...], turned_ref[...]).astype(BF16)
    for i, ref in enumerate((first_ref, second_ref)):
        ref[:, :known] = some_ref[i * half : (i + 1) * half, :]
        ref[:, known:] = value[i * half : (i + 1) * half]


def weight_products(grads, turned, kinds, share):
    blocks, slabs = len(grads) - 1, len(turned)
    tokens, width = turned[0].shape
    rows = kinds * share * blocks
    cost = dict(flops=2 * rows * tokens * width * slabs, bytes_accessed=4 * 2**20, transcendentals=0)
    left, some, own, filters = pl.pallas_call(
        functools.partial(product_kernel, kinds, share, blocks, slabs),
        out_shape=[
            jax.ShapeDtypeStruct((rows, tokens), BF16),
            jax.ShapeDtypeStruct((rows, width * slabs), BF16),
            jax.ShapeDtypeStruct((rows, tokens // blocks), BF16),
            jax.ShapeDtypeStruct((share * blocks, tokens // blocks), F32),
        ],
        in_specs=[VMEM] * (blocks + 1 + slabs),
        out_specs=[VMEM] * 4,
        compiler_params=pltpu.CompilerParams(vmem_limit_bytes=VMEM_BYTES),
        cost_estimate=pl.CostEstimate(**cost),
        name="products",
    )(*grads, *turned)
    return left, some, own, filters


def last_products(left, some, turned):
    rows, known = some.shape
    tokens, width = turned.shape
    half = jax.ShapeDtypeStruct((rows // 2, known + width), BF16)
    return pl.pallas_call(
        last_kernel,
        out_shape=[half, half],
        in_specs=[VMEM] * 3,
        out_specs=[VMEM] * 2,
        compiler_params=pltpu.CompilerParams(vmem_limit_bytes=VMEM_BYTES),
        cost_estimate=pl.CostEstimate(flops=2 * rows * tokens * width, bytes_accessed=2**20, transcendentals=0),
        name="products",
    )(left, some, turned)


def piece_kernel(values_ref, out_ref):
    width = out_ref.shape[2]
    for i in range(out_ref.shape[0]):
        out_ref[i] = values_ref[:, i * width : (i + 1) * width]


def column_pieces(values, blocks):
    rows, width = values.shape
    return pl.pallas_call(
        piece_kernel,
        out_shape=jax.ShapeDtypeStruct((blocks, rows, width // blocks), values.dtype),
        in_specs=[VMEM],
        out_specs=VMEM,
        compiler_params=pltpu.CompilerParams(vmem_limit_bytes=VMEM_BYTES),
        cost_estimate=pl.CostEstimate(flops=0, bytes_accessed=2**21, transcendentals=0),
        name="pieces",
    )(values)


def input_kernel(count, *refs):
    sums = 0.0
    for grad_ref, weight_ref in zip(refs[:count], refs[count : 2 * count]):
        sums = sums + lax.dot_general(
            grad_ref[...], weight_ref[...], (((0,), (0,)), ((), ())), preferred_element_type=F32
        )
    refs[-1][...] = sums.astype(BF16)


def input_gradient(grads, weights):
    rows, length = grads[0].shape
    width = weights[0].shape[1]
    return pl.pallas_call(
        functools.partial(input_kernel, len(grads)),
        out_shape=jax.ShapeDtypeStruct((length, width), BF16),
        in_specs=[VMEM] * (2 * len(grads)),
        out_specs=VMEM,
        compiler_params=pltpu.CompilerParams(vmem_limit_bytes=VMEM_BYTES),
        cost_estimate=pl.CostEstimate(
            flops=2 * rows * len(grads) * length * width, bytes_accessed=4 * 2**20, transcendentals=0
        ),
        name="inputs",
    )(*grads, *weights)


def place_kernel(kinds, share, factor, *refs):
    out_ref = refs[-1]
    blocks = (len(refs) - 1) // 2
    place = lax.axis_index("ctx")
    slab = lax.axis_index("chan") ^ pl.program_id(0)
    width = out_ref.shape[1] // blocks
    source = pl.ds(pl.multiple_of(slab * width, width), width)
    for a in range(2):
        for r in range(blocks):
            sender = lax.rem(place + (r if a else blocks - r), blocks)
            columns = pl.ds(pl.multiple_of(sender * width, width), width)
            for b in range(2):
                for k in range(kinds):
                    row = (b * kinds + k) * share
                    value = refs[a * blocks + r][row : row + share, source].astype(F32) * factor
                    to = pl.multiple_of(k * share * blocks + (sender ^ (2 * a + b)) * share, share)
                    out_ref[pl.ds(to, share), columns] = value


def place_weights(pieces, kinds, share, slabs, factor):
    flat = [piece for group in pieces for piece in group]
    depth = flat[0].shape[1]
    rows = kinds * share * len(pieces[0])
    return pl.pallas_call(
        functools.partial(place_kernel, kinds, share, factor),
        out_shape=jax.ShapeDtypeStruct((rows, depth * slabs), F32),
        grid=(slabs,),
        in_specs=[pl.BlockSpec(flat[0].shape, lambda i: (0, 0))] * len(flat),
        out_specs=pl.BlockSpec((rows, depth), lambda i: (0, i)),
        compiler_params=pltpu.CompilerParams(vmem_limit_bytes=VMEM_BYTES),
        cost_estimate=pl.CostEstimate(flops=0, bytes_accessed=6 * 2**20, transcendentals=0),
        name="place",
    )(*flat)


def swap(values, axis, mask):
    if mask == 0:
        return values
    size = lax.axis_size(axis)
    return lax.ppermute(values, axis, [(i, i ^ mask) for i in range(size)])


def after(values, *others):
    return lax.optimization_barrier((values, *others))[0]


def gather_chan(values):
    slabs = lax.axis_size("chan")
    if slabs != 4:
        return [swap(values, "chan", m) for m in range(slabs)]
    far = swap(values, "chan", 2)
    return [values, swap(values, "chan", 1), far, swap(far, "chan", 1)]


def ring(values, step):
    size = lax.axis_size("ctx")
    found = [values]
    while len(found) < size:
        found.append(lax.ppermute(found[-1], "ctx", [(i, (i + step) % size) for i in range(size)]))
    return found


def general_tail(messages, features, place, mine, kinds, share, factor):
    blocks = lax.axis_size("ctx")
    length, width = features[0].shape
    rows = kinds * share * blocks
    grad_proj = jnp.zeros((kinds, share * blocks, length), BF16)
    grad_filter = jnp.zeros((share * blocks, length), F32)
    for m, message in enumerate(messages):
        piece = lax.dynamic_slice_in_dim(message, (place ^ m) * length, length, 1)
        piece = swap(piece, "ctx", m).reshape(kinds, share, length)
        grad_proj = lax.dynamic_update_slice_in_dim(grad_proj, piece, (place ^ m) * share, 1)
        end = swap(message[:, blocks * length :], "ctx", m).astype(F32)
        end = jnp.concatenate([end[:share], end[2 * share :, : length // 4]], axis=1)
        grad_filter = lax.dynamic_update_slice_in_dim(grad_filter, end, (place ^ m) * share, 0)
    grad_proj = grad_proj.reshape(rows, length)
    grad_weight = jnp.zeros((rows, width * len(features)), F32)
    for m, slab in enumerate(features):
        total = lax.psum(mm(grad_proj, slab).astype(BF16), "ctx").astype(F32) * factor
        grad_weight = lax.dynamic_update_slice_in_dim(grad_weight, total, (mine ^ m) * width, 1)
    return grad_proj, grad_weight, grad_filter


def per_device(activations, proj_weight, long_filter, skip_gain, out_grad):
    blocks = lax.axis_size("ctx")
    slabs = lax.axis_size("chan")
    place = lax.axis_index("ctx")
    mine = lax.axis_index("chan")
    length, width = activations.shape
    kinds, own, depth = proj_weight.shape
    share = own // blocks
    factor = (length * blocks) ** (-0.5)
    rows = kinds * own
    line = blocks == 4 and slabs == 4 and width % (blocks * LANES) == 0 and share % 16 == 0
    weight_rows = proj_weight.reshape(rows, depth)

    def share_of(array, m, axis=0, size=share):
        return lax.dynamic_slice_in_dim(array, (place ^ m) * size, size, axis)

    if line:
        features = [activations, swap(activations, "chan", 1), swap(activations, "chan", 2)]
    else:
        features = [swap(activations, "chan", m) for m in range(slabs)]

    along = [out_grad.astype(F32), long_filter]
    gain = share_of(skip_gain, 0)[:, None]

    if line:
        turned = after(column_pieces(activations, blocks), features[1])
        turned = lax.all_to_all(turned, "ctx", split_axis=0, concat_axis=0).reshape(length * blocks, width // blocks)
        sums = project(weight_rows, [], features[:2], [0, 1])
        features[2], sums, along = lax.optimization_barrier((features[2], sums, along))
        features.append(swap(features[2], "chan", 1))
        sums = project(weight_rows, sums, features[2:3], [2])
        pieces = project(weight_rows, sums, features[3:], [3], (blocks, kinds, along))
    else:
        sums = project(weight_rows, [], features[:1], [0])
        pieces = project(weight_rows, sums, features[1:], list(range(1, slabs)), (blocks, kinds, along))
    signals = [swap(piece, "ctx", m) for m, piece in enumerate(pieces)]
    if line:
        signals, turned = lax.optimization_barrier((signals, turned))
        turned = [turned, swap(turned, "chan", 1), swap(turned, "chan", 2)]
    messages = convolve(signals, gain)
    weight_cols = [lax.dynamic_slice_in_dim(weight_rows, (mine ^ m) * width, width, 1) for m in range(slabs)]
    weight_cols = after(weight_cols, turned[2] if line else signals[-1])
    weight_cols = [swap(cols, "chan", m) for m, cols in enumerate(weight_cols)]

    if line:
        messages = [messages[0], swap(messages[1], "ctx", 1), swap(messages[2], "ctx", 2), messages[3]]
        messages[3] = lax.ppermute(messages[3], "ctx", [(1, 2), (2, 1)])
        messages.append(lax.ppermute(messages[2], "ctx", [(1, 0), (2, 3)]))
        far, messages = lax.optimization_barrier((turned[2], messages))
        far = swap(far, "chan", 1)
        left, some, grad_proj, grad_filter = weight_products(messages, turned, kinds, share)
        first, second = last_products(left, some, far)
        first, second, grad_proj = lax.optimization_barrier((first, second, grad_proj))
        pieces = [ring(first, 1), ring(second, -1)]
        gathered = gather_chan(grad_proj)
        grad_rows = input_gradient(gathered, weight_cols)
        grad_rows, pieces = lax.optimization_barrier((grad_rows, pieces))
        grad_weight = place_weights(pieces, kinds, share, slabs, factor)
    else:
        grad_proj, grad_weight, grad_filter = general_tail(messages, features, place, mine, kinds, share, factor)
        grad_rows = input_gradient(gather_chan(grad_proj), weight_cols)
    return (
        grad_rows,
        grad_weight.reshape(kinds, own, depth),
        grad_filter,
    )


def solution(mesh):
    placed = (
        P(("files", "ctx"), "chan"),
        P(None, "chan", None),
        P("chan", "ctx"),
        P("chan"),
        P("chan", ("files", "ctx")),
    )
    return jax.shard_map(
        per_device,
        mesh=mesh,
        in_specs=placed,
        out_specs=(
            P(("files", "ctx"), "chan"),
            P("files", "chan", None),
            P("chan", ("files", "ctx")),
        ),
        check_vma=False,
    )
```

```python
import functools
import math

import jax
import jax.numpy as jnp
import numpy as np
from jax import lax
from jax.experimental import pallas as pl
from jax.experimental.pallas import tpu as pltpu
from jax.sharding import PartitionSpec as P

LANES = 128
BF16 = jnp.bfloat16
F32 = jnp.float32
VMEM = pl.BlockSpec(memory_space=pltpu.VMEM)
ANY = pl.BlockSpec(memory_space=pl.ANY)
VMEM_BYTES = 16 * 2**20


def split_table(table):
    high = np.asarray(table, np.float32).astype(BF16)
    low = (np.asarray(table, np.float64) - high.astype(np.float64)).astype(BF16)
    return np.stack([high, low])


def fourier_tables(tokens, group):
    period = 2 * tokens
    rows = period // LANES
    used = rows // 2
    freqs = rows // 2 + 1
    part = -(-freqs * group // 8) * 8
    k1 = np.arange(freqs)
    n1 = np.arange(used)
    angle = 2.0 * math.pi * (np.outer(k1, n1) % rows) / rows
    eye = np.eye(group)
    forward = np.zeros((2 * part, used * group))
    forward[: freqs * group] = np.kron(np.cos(angle), eye)
    forward[part : part + freqs * group] = np.kron(-np.sin(angle), eye)
    weight = np.where((k1 == 0) | (k1 == rows // 2), 1.0, 2.0)[None, :] / period
    inverse = np.zeros((used * group, 2 * part))
    inverse[:, : freqs * group] = np.kron(np.cos(angle.T) * weight, eye)
    inverse[:, part : part + freqs * group] = np.kron(-np.sin(angle.T) * weight, eye)
    n2 = np.arange(LANES)
    turn = 2.0 * math.pi * np.outer(k1, n2) / period
    twiddle = np.zeros((2, part, LANES), np.float32)
    twiddle[0, : freqs * group] = np.repeat(np.cos(turn), group, axis=0)
    twiddle[1, : freqs * group] = np.repeat(np.sin(turn), group, axis=0)
    inner = 2.0 * math.pi * (np.outer(n2, n2) % LANES) / LANES
    cos, sin = np.cos(inner), np.sin(inner)
    second = np.block([[cos, -sin], [sin, cos]])
    second_back = np.block([[cos, sin], [-sin, cos]])
    return (
        split_table(forward),
        split_table(second),
        split_table(second_back),
        split_table(inverse),
        twiddle,
    )


def halves(values):
    high = values.astype(BF16)
    return high, (values - high.astype(F32)).astype(BF16)


def mm(left, right):
    return jnp.dot(left, right, preferred_element_type=F32)


def table_left(table, values):
    high, low = halves(values)
    return mm(table[0], high) + (mm(table[0], low) + mm(table[1], high))


def table_right(values, table):
    high, low = halves(values)
    return mm(high, table[0]) + (mm(low, table[0]) + mm(high, table[1]))


def conv_kernel(blocks, chans, group, factor, *refs):
    count = blocks + 5
    gain_ref, sources, refs = refs[0], refs[1 : 1 + count], refs[1 + count :]
    out_refs = refs[:blocks]
    series, results, inputs = refs[blocks : 3 + blocks]
    held = refs[3 + blocks : 3 + blocks + count]
    sems = refs[3 + blocks + count]
    copies = [pltpu.make_async_copy(sources[i], held[i], sems.at[i]) for i in range(count)]
    for copy in copies:
        copy.start()
    signal_refs = held[:blocks]
    fwd_ref, second_ref, back_ref, inv_ref, twiddle_ref = held[blocks:]
    place = lax.axis_index("ctx")
    length = series.shape[-1]
    cuts = length // LANES
    for m in range(blocks):
        where = place ^ m
        copies[m].wait()
        values = signal_refs[m][...].astype(F32)
        upstream = values[3 * chans : 4 * chans]
        inputs[0, where] = values[:chans]
        inputs[1, where] = values[2 * chans : 3 * chans]
        inputs[2, where] = upstream
        series[0, where] = values[4 * chans :] * factor
        series[1, where] = values[:chans] * values[2 * chans : 3 * chans]
        series[2, where] = upstream * values[chans : 2 * chans]
    for copy in copies[blocks:]:
        copy.wait()
    part = twiddle_ref.shape[1]
    cos, sin = twiddle_ref[0], twiddle_ref[1]
    for start in range(0, chans, group):
        picked = []
        for q in range(3):
            tiles = []
            for z in range(blocks):
                loaded = series[q, z]
                loaded = loaded[start : start + group]
                for n in range(cuts):
                    tiles.append(loaded[:, n * LANES : (n + 1) * LANES])
            picked.append(jnp.concatenate(tiles, axis=0))
        first = table_left(fwd_ref, jnp.concatenate(picked, axis=1))
        turned = []
        for q in range(3):
            re = first[:part, q * LANES : (q + 1) * LANES]
            im = first[part:, q * LANES : (q + 1) * LANES]
            turned.append(jnp.concatenate([re * cos + im * sin, im * cos - re * sin], axis=1))
        spectra = table_right(jnp.concatenate(turned, axis=0), second_ref)
        parts = [
            (spectra[q * part : (q + 1) * part, :LANES], spectra[q * part : (q + 1) * part, LANES:])
            for q in range(3)
        ]
        (fr, fi), (gr, gi), (ur, ui) = parts
        products = jnp.concatenate(
            [
                jnp.concatenate([fr * gr - fi * gi, fr * gi + fi * gr], axis=1),
                jnp.concatenate([fr * ur + fi * ui, fr * ui - fi * ur], axis=1),
                jnp.concatenate([gr * ur + gi * ui, gr * ui - gi * ur], axis=1),
            ],
            axis=0,
        )
        back = table_right(products, back_ref)
        turned = []
        for q in range(3):
            re = back[q * part : (q + 1) * part, :LANES]
            im = back[q * part : (q + 1) * part, LANES:]
            turned.append(jnp.concatenate([re * cos - im * sin, im * cos + re * sin], axis=0))
        final = table_left(inv_ref, jnp.concatenate(turned, axis=1))
        for q in range(3):
            for z in range(blocks):
                tiles = [
                    final[(z * cuts + n) * group : (z * cuts + n + 1) * group, q * LANES : (q + 1) * LANES]
                    for n in range(cuts)
                ]
                results[q, z, start : start + group, :] = jnp.concatenate(tiles, axis=1)
    gain = gain_ref[...]
    for z in range(blocks):
        conv_out = results[0, z] + gain * series[1, z]
        grad_gated = results[1, z] + gain * series[2, z]
        grads = jnp.concatenate(
            [grad_gated * inputs[1, z], inputs[2, z] * conv_out, grad_gated * inputs[0, z]], axis=0
        ).astype(BF16)
        for ref in out_refs:
            ref[:, z * length : (z + 1) * length] = grads
    found = [(factor * results[2, place ^ m]).astype(BF16).astype(F32) for m in range(blocks)]
    cut = 3 * length // 4
    rest = jnp.zeros((chans, length - cut), F32)
    for m in range(blocks):
        pair = found[m], found[min(m ^ 1, blocks - 1)]
        last = jnp.concatenate([pair[0][:, cut:], pair[1][:, cut:], rest], axis=1)
        rows = jnp.concatenate([pair[0][:, :cut], pair[1][:, :cut], last], axis=0)
        out_refs[m][:, blocks * length :] = rows.astype(BF16)


def convolve(signals, gain):
    blocks = len(signals)
    chans, length = signals[0].shape[0] // 5, signals[0].shape[1]
    tokens = blocks * length
    group = max(1, min(chans, 8, LANES * LANES // tokens))
    tables = fourier_tables(tokens, group)
    arrays = [*signals, *[jnp.asarray(table) for table in tables]]
    part = tables[4].shape[1]
    flops = 2 * 3 * (chans // group) * 3 * (4 * part * group * (tokens // LANES) * LANES + 2 * part * 256 * 256)
    return pl.pallas_call(
        functools.partial(conv_kernel, blocks, chans, group, tokens ** (-0.5)),
        out_shape=[jax.ShapeDtypeStruct((3 * chans, tokens + 3 * length // 4), BF16)] * blocks,
        in_specs=[VMEM] + [ANY] * len(arrays),
        out_specs=[VMEM] * blocks,
        scratch_shapes=[pltpu.VMEM((3, blocks, chans, length), F32)] * 3
        + [pltpu.VMEM(array.shape, array.dtype) for array in arrays]
        + [pltpu.SemaphoreType.DMA((len(arrays),))],
        compiler_params=pltpu.CompilerParams(vmem_limit_bytes=60 * 2**20),
        cost_estimate=pl.CostEstimate(flops=flops, bytes_accessed=4 * 2**20, transcendentals=0),
        name="conv",
    )(gain, *arrays)


def partial_rows(weight_ref, refs, masks):
    mine = lax.axis_index("chan")
    sums = 0.0
    for m, ref in zip(masks, refs):
        width = ref.shape[1]
        at = pl.multiple_of((mine ^ m) * width, width)
        sums = sums + lax.dot_general(
            ref[...], weight_ref[:, pl.ds(at, width)], (((1,), (1,)), ((), ())), preferred_element_type=F32
        )
    return sums


def start_kernel(masks, weight_ref, *refs):
    refs[-1][...] = partial_rows(weight_ref, refs[:-1], masks)


def more_kernel(masks, weight_ref, sum_ref, *refs):
    refs[-1][...] = sum_ref[...] + partial_rows(weight_ref, refs[:-1], masks)


def finish_kernel(masks, blocks, kinds, share, given_ref, filter_ref, weight_ref, sum_ref, *refs):
    out_refs = refs[len(masks) : len(masks) + blocks]
    total = refs[-1]
    place = lax.axis_index("ctx")
    total[...] = (sum_ref[...] + partial_rows(weight_ref, refs[: len(masks)], masks)).T
    for m in range(blocks):
        first = (place ^ m) * share
        rows = [total[pl.ds(pl.multiple_of(k * share * blocks + first, share), share), :] for k in range(kinds)]
        for ref in (given_ref, filter_ref):
            rows.append(ref[pl.ds(pl.multiple_of(first, share), share), :])
        out_refs[m][...] = jnp.concatenate(rows, axis=0).astype(BF16)


def project(weight_rows, sums, features, masks, out=None):
    rows, depth = weight_rows.shape
    length, width = features[0].shape
    along = []
    if out is None:
        body = functools.partial(more_kernel if sums else start_kernel, masks)
        shape = [jax.ShapeDtypeStruct((length, rows), F32)]
    else:
        blocks, kinds, along = out
        share = rows // kinds // blocks
        body = functools.partial(finish_kernel, masks, blocks, kinds, share)
        shape = [jax.ShapeDtypeStruct(((kinds + 2) * share, length), BF16)] * blocks
    flops = 2 * rows * length * width * len(masks)
    return pl.pallas_call(
        body,
        out_shape=shape,
        in_specs=[VMEM] * (len(along) + 1 + len(sums) + len(features)),
        out_specs=[VMEM] * len(shape),
        scratch_shapes=[pltpu.VMEM((rows, length), F32)] if out else [],
        compiler_params=pltpu.CompilerParams(vmem_limit_bytes=VMEM_BYTES),
        cost_estimate=pl.CostEstimate(flops=flops, bytes_accessed=2**20, transcendentals=0),
        name="project",
    )(*along, weight_rows, *sums, *features)


def product_kernel(kinds, share, blocks, slabs, *refs):
    grad_refs, turned = refs[: blocks + 1], refs[blocks + 1 : blocks + 1 + slabs]
    left_ref, some_ref, own_ref, filter_ref = refs[blocks + 1 + slabs :]
    place = lax.axis_index("ctx")
    length = own_ref.shape[1]
    width = turned[0].shape[1]
    rows = kinds * share
    tokens = blocks * length
    mine = pl.ds(pl.multiple_of(place * length, length), length)
    middle = (place == 1) | (place == 2)
    for m in range(blocks):
        value = grad_refs[m][:, :tokens]
        if m == blocks - 1:
            value = value + grad_refs[blocks][:, :tokens]
        left_ref[m * rows : (m + 1) * rows, :] = value
        for k in range(kinds):
            to = pl.multiple_of(k * share * blocks + (place ^ m) * share, share)
            own_ref[pl.ds(to, share), :] = left_ref[m * rows + k * share : m * rows + (k + 1) * share, mine]
        end = grad_refs[m][:, tokens:].astype(F32)
        cut = end.shape[1]
        size = length - cut
        given = jnp.concatenate([end[:share], end[2 * share :, :size]], axis=1)
        if m == blocks - 1:
            end = grad_refs[blocks][:, tokens:].astype(F32)
            handed = jnp.concatenate([end[share : 2 * share], end[2 * share :, size : 2 * size]], axis=1)
            given = jnp.where(middle, given, handed)
        to = pl.multiple_of((place ^ m) * share, share)
        filter_ref[pl.ds(to, share), :] = given
    for i in range(slabs):
        some_ref[:, i * width : (i + 1) * width] = mm(left_ref[...], turned[i][...]).astype(BF16)


def last_kernel(left_ref, some_ref, turned_ref, first_ref, second_ref):
    half, known = first_ref.shape[0], some_ref.shape[1]
    value = mm(left_ref[...], turned_ref[...]).astype(BF16)
    for i, ref in enumerate((first_ref, second_ref)):
        ref[:, :known] = some_ref[i * half : (i + 1) * half, :]
        ref[:, known:] = value[i * half : (i + 1) * half]


def weight_products(grads, turned, kinds, share):
    blocks, slabs = len(grads) - 1, len(turned)
    tokens, width = turned[0].shape
    rows = kinds * share * blocks
    cost = dict(flops=2 * rows * tokens * width * slabs, bytes_accessed=4 * 2**20, transcendentals=0)
    left, some, own, filters = pl.pallas_call(
        functools.partial(product_kernel, kinds, share, blocks, slabs),
        out_shape=[
            jax.ShapeDtypeStruct((rows, tokens), BF16),
            jax.ShapeDtypeStruct((rows, width * slabs), BF16),
            jax.ShapeDtypeStruct((rows, tokens // blocks), BF16),
            jax.ShapeDtypeStruct((share * blocks, tokens // blocks), F32),
        ],
        in_specs=[VMEM] * (blocks + 1 + slabs),
        out_specs=[VMEM] * 4,
        compiler_params=pltpu.CompilerParams(vmem_limit_bytes=VMEM_BYTES),
        cost_estimate=pl.CostEstimate(**cost),
        name="products",
    )(*grads, *turned)
    return left, some, own, filters


def last_products(left, some, turned):
    rows, known = some.shape
    tokens, width = turned.shape
    half = jax.ShapeDtypeStruct((rows // 2, known + width), BF16)
    return pl.pallas_call(
        last_kernel,
        out_shape=[half, half],
        in_specs=[VMEM] * 3,
        out_specs=[VMEM] * 2,
        compiler_params=pltpu.CompilerParams(vmem_limit_bytes=VMEM_BYTES),
        cost_estimate=pl.CostEstimate(flops=2 * rows * tokens * width, bytes_accessed=2**20, transcendentals=0),
        name="products",
    )(left, some, turned)


def piece_kernel(values_ref, out_ref):
    width = out_ref.shape[2]
    for i in range(out_ref.shape[0]):
        out_ref[i] = values_ref[:, i * width : (i + 1) * width]


def column_pieces(values, blocks):
    rows, width = values.shape
    return pl.pallas_call(
        piece_kernel,
        out_shape=jax.ShapeDtypeStruct((blocks, rows, width // blocks), values.dtype),
        in_specs=[VMEM],
        out_specs=VMEM,
        compiler_params=pltpu.CompilerParams(vmem_limit_bytes=VMEM_BYTES),
        cost_estimate=pl.CostEstimate(flops=0, bytes_accessed=2**21, transcendentals=0),
        name="pieces",
    )(values)


def input_kernel(count, *refs):
    sums = 0.0
    for grad_ref, weight_ref in zip(refs[:count], refs[count : 2 * count]):
        sums = sums + lax.dot_general(
            grad_ref[...], weight_ref[...], (((0,), (0,)), ((), ())), preferred_element_type=F32
        )
    refs[-1][...] = sums.astype(BF16)


def input_gradient(grads, weights):
    rows, length = grads[0].shape
    width = weights[0].shape[1]
    return pl.pallas_call(
        functools.partial(input_kernel, len(grads)),
        out_shape=jax.ShapeDtypeStruct((length, width), BF16),
        in_specs=[VMEM] * (2 * len(grads)),
        out_specs=VMEM,
        compiler_params=pltpu.CompilerParams(vmem_limit_bytes=VMEM_BYTES),
        cost_estimate=pl.CostEstimate(
            flops=2 * rows * len(grads) * length * width, bytes_accessed=4 * 2**20, transcendentals=0
        ),
        name="inputs",
    )(*grads, *weights)


def place_kernel(kinds, share, factor, *refs):
    out_ref = refs[-1]
    blocks = (len(refs) - 1) // 2
    place = lax.axis_index("ctx")
    slab = lax.axis_index("chan") ^ pl.program_id(0)
    width = out_ref.shape[1] // blocks
    source = pl.ds(pl.multiple_of(slab * width, width), width)
    for a in range(2):
        for r in range(blocks):
            sender = lax.rem(place + (r if a else blocks - r), blocks)
            columns = pl.ds(pl.multiple_of(sender * width, width), width)
            for b in range(2):
                for k in range(kinds):
                    row = (b * kinds + k) * share
                    value = refs[a * blocks + r][row : row + share, source].astype(F32) * factor
                    to = pl.multiple_of(k * share * blocks + (sender ^ (2 * a + b)) * share, share)
                    out_ref[pl.ds(to, share), columns] = value


def place_weights(pieces, kinds, share, slabs, factor):
    flat = [piece for group in pieces for piece in group]
    depth = flat[0].shape[1]
    rows = kinds * share * len(pieces[0])
    return pl.pallas_call(
        functools.partial(place_kernel, kinds, share, factor),
        out_shape=jax.ShapeDtypeStruct((rows, depth * slabs), F32),
        grid=(slabs,),
        in_specs=[pl.BlockSpec(flat[0].shape, lambda i: (0, 0))] * len(flat),
        out_specs=pl.BlockSpec((rows, depth), lambda i: (0, i)),
        compiler_params=pltpu.CompilerParams(vmem_limit_bytes=VMEM_BYTES),
        cost_estimate=pl.CostEstimate(flops=0, bytes_accessed=6 * 2**20, transcendentals=0),
        name="place",
    )(*flat)


def swap(values, axis, mask):
    if mask == 0:
        return values
    size = lax.axis_size(axis)
    return lax.ppermute(values, axis, [(i, i ^ mask) for i in range(size)])


def after(values, *others):
    return lax.optimization_barrier((values, *others))[0]


def gather_chan(values):
    slabs = lax.axis_size("chan")
    if slabs != 4:
        return [swap(values, "chan", m) for m in range(slabs)]
    far = swap(values, "chan", 2)
    return [values, swap(values, "chan", 1), far, swap(far, "chan", 1)]


def ring(values, step):
    size = lax.axis_size("ctx")
    found = [values]
    while len(found) < size:
        found.append(lax.ppermute(found[-1], "ctx", [(i, (i + step) % size) for i in range(size)]))
    return found


def general_tail(messages, features, place, mine, kinds, share, factor):
    blocks = lax.axis_size("ctx")
    length, width = features[0].shape
    rows = kinds * share * blocks
    grad_proj = jnp.zeros((kinds, share * blocks, length), BF16)
    grad_filter = jnp.zeros((share * blocks, length), F32)
    for m, message in enumerate(messages):
        piece = lax.dynamic_slice_in_dim(message, (place ^ m) * length, length, 1)
        piece = swap(piece, "ctx", m).reshape(kinds, share, length)
        grad_proj = lax.dynamic_update_slice_in_dim(grad_proj, piece, (place ^ m) * share, 1)
        end = swap(message[:, blocks * length :], "ctx", m).astype(F32)
        end = jnp.concatenate([end[:share], end[2 * share :, : length // 4]], axis=1)
        grad_filter = lax.dynamic_update_slice_in_dim(grad_filter, end, (place ^ m) * share, 0)
    grad_proj = grad_proj.reshape(rows, length)
    grad_weight = jnp.zeros((rows, width * len(features)), F32)
    for m, slab in enumerate(features):
        total = lax.psum(mm(grad_proj, slab).astype(BF16), "ctx").astype(F32) * factor
        grad_weight = lax.dynamic_update_slice_in_dim(grad_weight, total, (mine ^ m) * width, 1)
    return grad_proj, grad_weight, grad_filter


def per_device(activations, proj_weight, long_filter, skip_gain, out_grad):
    blocks = lax.axis_size("ctx")
    slabs = lax.axis_size("chan")
    place = lax.axis_index("ctx")
    mine = lax.axis_index("chan")
    length, width = activations.shape
    kinds, own, depth = proj_weight.shape
    share = own // blocks
    factor = (length * blocks) ** (-0.5)
    rows = kinds * own
    line = blocks == 4 and slabs == 4 and width % (blocks * LANES) == 0 and share % 16 == 0
    weight_rows = proj_weight.reshape(rows, depth)

    def share_of(array, m, axis=0, size=share):
        return lax.dynamic_slice_in_dim(array, (place ^ m) * size, size, axis)

    if line:
        features = [activations, swap(activations, "chan", 1), swap(activations, "chan", 2)]
    else:
        features = [swap(activations, "chan", m) for m in range(slabs)]

    along = [out_grad.astype(F32), long_filter]
    gain = share_of(skip_gain, 0)[:, None]

    weight_cols = [lax.dynamic_slice_in_dim(weight_rows, (mine ^ m) * width, width, 1) for m in range(slabs)]
    if line:
        turned = after(column_pieces(activations, blocks), features[1])
        turned = lax.all_to_all(turned, "ctx", split_axis=0, concat_axis=0).reshape(length * blocks, width // blocks)
        sums = project(weight_rows, [], features[:2], [0, 1])
        weight_cols[1] = swap(weight_cols[1], "chan", 1)
        features[2], sums, along, gain, weight_cols = lax.optimization_barrier(
            (features[2], sums, along, gain, weight_cols)
        )
        features.append(swap(features[2], "chan", 1))
        sums = project(weight_rows, sums, features[2:3], [2])
        pieces = project(weight_rows, sums, features[3:], [3], (blocks, kinds, along))
    else:
        sums = project(weight_rows, [], features[:1], [0])
        pieces = project(weight_rows, sums, features[1:], list(range(1, slabs)), (blocks, kinds, along))
    signals = [swap(piece, "ctx", m) for m, piece in enumerate(pieces)]
    if line:
        signals, turned = lax.optimization_barrier((signals, turned))
        turned = [turned, swap(turned, "chan", 1), swap(turned, "chan", 2)]
    messages = convolve(signals, gain)

    if line:
        messages = [messages[0], swap(messages[1], "ctx", 1), swap(messages[2], "ctx", 2), messages[3]]
        messages[3] = lax.ppermute(messages[3], "ctx", [(1, 2), (2, 1)])
        messages.append(lax.ppermute(messages[2], "ctx", [(1, 0), (2, 3)]))
        far, messages = lax.optimization_barrier((turned[2], messages))
        far = swap(far, "chan", 1)
        left, some, grad_proj, grad_filter = weight_products(messages, turned, kinds, share)
        first, second = last_products(left, some, far)
        first, second, grad_proj = lax.optimization_barrier((first, second, grad_proj))
        pieces = [ring(first, 1), ring(second, -1)]
        gathered = gather_chan(grad_proj)
        weight_cols = after(weight_cols, gathered[2])
        weight_cols = [*weight_cols[:2], swap(weight_cols[2], "chan", 2), swap(weight_cols[3], "chan", 3)]
        grad_rows = input_gradient(gathered, weight_cols)
        grad_rows, pieces = lax.optimization_barrier((grad_rows, pieces))
        grad_weight = place_weights(pieces, kinds, share, slabs, factor)
    else:
        grad_proj, grad_weight, grad_filter = general_tail(messages, features, place, mine, kinds, share, factor)
        weight_cols = [swap(cols, "chan", m) for m, cols in enumerate(weight_cols)]
        grad_rows = input_gradient(gather_chan(grad_proj), weight_cols)
    return (
        grad_rows,
        grad_weight.reshape(kinds, own, depth),
        grad_filter,
    )


def solution(mesh):
    placed = (
        P(("files", "ctx"), "chan"),
        P(None, "chan", None),
        P("chan", "ctx"),
        P("chan"),
        P("chan", ("files", "ctx")),
    )
    return jax.shard_map(
        per_device,
        mesh=mesh,
        in_specs=placed,
        out_specs=(
            P(("files", "ctx"), "chan"),
            P("files", "chan", None),
            P("chan", ("files", "ctx")),
        ),
        check_vma=False,
    )
```

```python
import functools
import math

import jax
import jax.numpy as jnp
import numpy as np
from jax import lax
from jax.experimental import pallas as pl
from jax.experimental.pallas import tpu as pltpu
from jax.sharding import PartitionSpec as P

LANES = 128
BF16 = jnp.bfloat16
F32 = jnp.float32
VMEM = pl.BlockSpec(memory_space=pltpu.VMEM)
ANY = pl.BlockSpec(memory_space=pl.ANY)
VMEM_BYTES = 16 * 2**20


def split_table(table):
    high = np.asarray(table, np.float32).astype(BF16)
    low = (np.asarray(table, np.float64) - high.astype(np.float64)).astype(BF16)
    return np.stack([high, low])


def fourier_tables(tokens, group):
    period = 2 * tokens
    rows = period // LANES
    used = rows // 2
    freqs = rows // 2 + 1
    part = -(-freqs * group // 8) * 8
    k1 = np.arange(freqs)
    n1 = np.arange(used)
    angle = 2.0 * math.pi * (np.outer(k1, n1) % rows) / rows
    eye = np.eye(group)
    forward = np.zeros((2 * part, used * group))
    forward[: freqs * group] = np.kron(np.cos(angle), eye)
    forward[part : part + freqs * group] = np.kron(-np.sin(angle), eye)
    weight = np.where((k1 == 0) | (k1 == rows // 2), 1.0, 2.0)[None, :] / period
    inverse = np.zeros((used * group, 2 * part))
    inverse[:, : freqs * group] = np.kron(np.cos(angle.T) * weight, eye)
    inverse[:, part : part + freqs * group] = np.kron(-np.sin(angle.T) * weight, eye)
    n2 = np.arange(LANES)
    turn = 2.0 * math.pi * np.outer(k1, n2) / period
    twiddle = np.zeros((2, part, LANES), np.float32)
    twiddle[0, : freqs * group] = np.repeat(np.cos(turn), group, axis=0)
    twiddle[1, : freqs * group] = np.repeat(np.sin(turn), group, axis=0)
    inner = 2.0 * math.pi * (np.outer(n2, n2) % LANES) / LANES
    cos, sin = np.cos(inner), np.sin(inner)
    second = np.block([[cos, -sin], [sin, cos]])
    second_back = np.block([[cos, sin], [-sin, cos]])
    return (
        split_table(forward),
        split_table(second),
        split_table(second_back),
        split_table(inverse),
        twiddle,
    )


def halves(values):
    high = values.astype(BF16)
    return high, (values - high.astype(F32)).astype(BF16)


def mm(left, right):
    return jnp.dot(left, right, preferred_element_type=F32)


def table_left(table, values):
    high, low = halves(values)
    return mm(table[0], high) + (mm(table[0], low) + mm(table[1], high))


def table_right(values, table):
    high, low = halves(values)
    return mm(high, table[0]) + (mm(low, table[0]) + mm(high, table[1]))


def conv_kernel(blocks, chans, group, factor, *refs):
    count = blocks + 5
    gain_ref, sources, refs = refs[0], refs[1 : 1 + count], refs[1 + count :]
    out_refs = refs[:blocks]
    series, results, inputs = refs[blocks : 3 + blocks]
    held = refs[3 + blocks : 3 + blocks + count]
    sems = refs[3 + blocks + count]
    copies = [pltpu.make_async_copy(sources[i], held[i], sems.at[i]) for i in range(count)]
    for copy in copies:
        copy.start()
    signal_refs = held[:blocks]
    fwd_ref, second_ref, back_ref, inv_ref, twiddle_ref = held[blocks:]
    place = lax.axis_index("ctx")
    length = series.shape[-1]
    cuts = length // LANES
    for m in range(blocks):
        where = place ^ m
        copies[m].wait()
        values = signal_refs[m][...].astype(F32)
        upstream = values[3 * chans : 4 * chans]
        inputs[0, where] = values[:chans]
        inputs[1, where] = values[2 * chans : 3 * chans]
        inputs[2, where] = upstream
        series[0, where] = values[4 * chans :] * factor
        series[1, where] = values[:chans] * values[2 * chans : 3 * chans]
        series[2, where] = upstream * values[chans : 2 * chans]
    for copy in copies[blocks:]:
        copy.wait()
    part = twiddle_ref.shape[1]
    cos, sin = twiddle_ref[0], twiddle_ref[1]
    for start in range(0, chans, group):
        picked = []
        for q in range(3):
            tiles = []
            for z in range(blocks):
                loaded = series[q, z]
                loaded = loaded[start : start + group]
                for n in range(cuts):
                    tiles.append(loaded[:, n * LANES : (n + 1) * LANES])
            picked.append(jnp.concatenate(tiles, axis=0))
        first = table_left(fwd_ref, jnp.concatenate(picked, axis=1))
        turned = []
        for q in range(3):
            re = first[:part, q * LANES : (q + 1) * LANES]
            im = first[part:, q * LANES : (q + 1) * LANES]
            turned.append(jnp.concatenate([re * cos + im * sin, im * cos - re * sin], axis=1))
        spectra = table_right(jnp.concatenate(turned, axis=0), second_ref)
        parts = [
            (spectra[q * part : (q + 1) * part, :LANES], spectra[q * part : (q + 1) * part, LANES:])
            for q in range(3)
        ]
        (fr, fi), (gr, gi), (ur, ui) = parts
        products = jnp.concatenate(
            [
                jnp.concatenate([fr * gr - fi * gi, fr * gi + fi * gr], axis=1),
                jnp.concatenate([fr * ur + fi * ui, fr * ui - fi * ur], axis=1),
                jnp.concatenate([gr * ur + gi * ui, gr * ui - gi * ur], axis=1),
            ],
            axis=0,
        )
        back = table_right(products, back_ref)
        turned = []
        for q in range(3):
            re = back[q * part : (q + 1) * part, :LANES]
            im = back[q * part : (q + 1) * part, LANES:]
            turned.append(jnp.concatenate([re * cos - im * sin, im * cos + re * sin], axis=0))
        final = table_left(inv_ref, jnp.concatenate(turned, axis=1))
        for q in range(3):
            for z in range(blocks):
                tiles = [
                    final[(z * cuts + n) * group : (z * cuts + n + 1) * group, q * LANES : (q + 1) * LANES]
                    for n in range(cuts)
                ]
                results[q, z, start : start + group, :] = jnp.concatenate(tiles, axis=1)
    down = lax.broadcasted_iota(jnp.int32, (chans, chans), 0)
    along = lax.broadcasted_iota(jnp.int32, (chans, chans), 1)
    gain = jnp.sum(jnp.where(down == along, gain_ref[...], 0.0), axis=1, keepdims=True)
    for z in range(blocks):
        conv_out = results[0, z] + gain * series[1, z]
        grad_gated = results[1, z] + gain * series[2, z]
        grads = jnp.concatenate(
            [grad_gated * inputs[1, z], inputs[2, z] * conv_out, grad_gated * inputs[0, z]], axis=0
        ).astype(BF16)
        for ref in out_refs:
            ref[:, z * length : (z + 1) * length] = grads
    found = [(factor * results[2, place ^ m]).astype(BF16).astype(F32) for m in range(blocks)]
    cut = 3 * length // 4
    rest = jnp.zeros((chans, length - cut), F32)
    for m in range(blocks):
        pair = found[m], found[min(m ^ 1, blocks - 1)]
        last = jnp.concatenate([pair[0][:, cut:], pair[1][:, cut:], rest], axis=1)
        rows = jnp.concatenate([pair[0][:, :cut], pair[1][:, :cut], last], axis=0)
        out_refs[m][:, blocks * length :] = rows.astype(BF16)


def convolve(signals, gain):
    blocks = len(signals)
    chans, length = signals[0].shape[0] // 5, signals[0].shape[1]
    tokens = blocks * length
    group = max(1, min(chans, 8, LANES * LANES // tokens))
    tables = fourier_tables(tokens, group)
    arrays = [*signals, *[jnp.asarray(table) for table in tables]]
    part = tables[4].shape[1]
    flops = 2 * 3 * (chans // group) * 3 * (4 * part * group * (tokens // LANES) * LANES + 2 * part * 256 * 256)
    return pl.pallas_call(
        functools.partial(conv_kernel, blocks, chans, group, tokens ** (-0.5)),
        out_shape=[jax.ShapeDtypeStruct((3 * chans, tokens + 3 * length // 4), BF16)] * blocks,
        in_specs=[VMEM] + [ANY] * len(arrays),
        out_specs=[VMEM] * blocks,
        scratch_shapes=[pltpu.VMEM((3, blocks, chans, length), F32)] * 3
        + [pltpu.VMEM(array.shape, array.dtype) for array in arrays]
        + [pltpu.SemaphoreType.DMA((len(arrays),))],
        compiler_params=pltpu.CompilerParams(vmem_limit_bytes=60 * 2**20),
        cost_estimate=pl.CostEstimate(flops=flops, bytes_accessed=4 * 2**20, transcendentals=0),
        name="conv",
    )(gain, *arrays)


def partial_rows(weight_ref, refs, masks):
    mine = lax.axis_index("chan")
    sums = 0.0
    for m, ref in zip(masks, refs):
        width = ref.shape[1]
        at = pl.multiple_of((mine ^ m) * width, width)
        sums = sums + lax.dot_general(
            ref[...], weight_ref[:, pl.ds(at, width)], (((1,), (1,)), ((), ())), preferred_element_type=F32
        )
    return sums


def start_kernel(masks, weight_ref, *refs):
    refs[-1][...] = partial_rows(weight_ref, refs[:-1], masks)


def more_kernel(masks, weight_ref, sum_ref, *refs):
    refs[-1][...] = sum_ref[...] + partial_rows(weight_ref, refs[:-1], masks)


def finish_kernel(masks, blocks, kinds, share, given_ref, filter_ref, weight_ref, sum_ref, *refs):
    out_refs = refs[len(masks) : len(masks) + blocks]
    total = refs[-1]
    place = lax.axis_index("ctx")
    total[...] = (sum_ref[...] + partial_rows(weight_ref, refs[: len(masks)], masks)).T
    for m in range(blocks):
        first = (place ^ m) * share
        rows = [total[pl.ds(pl.multiple_of(k * share * blocks + first, share), share), :] for k in range(kinds)]
        for ref in (given_ref, filter_ref):
            rows.append(ref[pl.ds(pl.multiple_of(first, share), share), :])
        out_refs[m][...] = jnp.concatenate(rows, axis=0).astype(BF16)


def project(weight_rows, sums, features, masks, out=None):
    rows, depth = weight_rows.shape
    length, width = features[0].shape
    along = []
    if out is None:
        body = functools.partial(more_kernel if sums else start_kernel, masks)
        shape = [jax.ShapeDtypeStruct((length, rows), F32)]
    else:
        blocks, kinds, along = out
        share = rows // kinds // blocks
        body = functools.partial(finish_kernel, masks, blocks, kinds, share)
        shape = [jax.ShapeDtypeStruct(((kinds + 2) * share, length), BF16)] * blocks
    flops = 2 * rows * length * width * len(masks)
    return pl.pallas_call(
        body,
        out_shape=shape,
        in_specs=[VMEM] * (len(along) + 1 + len(sums) + len(features)),
        out_specs=[VMEM] * len(shape),
        scratch_shapes=[pltpu.VMEM((rows, length), F32)] if out else [],
        compiler_params=pltpu.CompilerParams(vmem_limit_bytes=VMEM_BYTES),
        cost_estimate=pl.CostEstimate(flops=flops, bytes_accessed=2**20, transcendentals=0),
        name="project",
    )(*along, weight_rows, *sums, *features)


def product_kernel(kinds, share, blocks, slabs, *refs):
    grad_refs, turned = refs[: blocks + 1], refs[blocks + 1 : blocks + 1 + slabs]
    left_ref, some_ref, own_ref, filter_ref = refs[blocks + 1 + slabs :]
    place = lax.axis_index("ctx")
    length = own_ref.shape[1]
    width = turned[0].shape[1]
    rows = kinds * share
    tokens = blocks * length
    mine = pl.ds(pl.multiple_of(place * length, length), length)
    middle = (place == 1) | (place == 2)
    for m in range(blocks):
        value = grad_refs[m][:, :tokens]
        if m == blocks - 1:
            value = jnp.where(middle, value, grad_refs[blocks][:, :tokens])
        left_ref[m * rows : (m + 1) * rows, :] = value
        for k in range(kinds):
            to = pl.multiple_of(k * share * blocks + (place ^ m) * share, share)
            own_ref[pl.ds(to, share), :] = left_ref[m * rows + k * share : m * rows + (k + 1) * share, mine]
        end = grad_refs[m][:, tokens:].astype(F32)
        cut = end.shape[1]
        size = length - cut
        given = jnp.concatenate([end[:share], end[2 * share :, :size]], axis=1)
        if m == blocks - 1:
            end = grad_refs[blocks][:, tokens:].astype(F32)
            handed = jnp.concatenate([end[share : 2 * share], end[2 * share :, size : 2 * size]], axis=1)
            given = jnp.where(middle, given, handed)
        to = pl.multiple_of((place ^ m) * share, share)
        filter_ref[pl.ds(to, share), :] = given
    for i in range(slabs):
        some_ref[:, i * width : (i + 1) * width] = mm(left_ref[...], turned[i][...]).astype(BF16)


def last_kernel(left_ref, some_ref, turned_ref, first_ref, second_ref):
    half, known = first_ref.shape[0], some_ref.shape[1]
    value = mm(left_ref[...], turned_ref[...]).astype(BF16)
    for i, ref in enumerate((first_ref, second_ref)):
        ref[:, :known] = some_ref[i * half : (i + 1) * half, :]
        ref[:, known:] = value[i * half : (i + 1) * half]


def weight_products(grads, turned, kinds, share):
    blocks, slabs = len(grads) - 1, len(turned)
    tokens, width = turned[0].shape
    rows = kinds * share * blocks
    cost = dict(flops=2 * rows * tokens * width * slabs, bytes_accessed=4 * 2**20, transcendentals=0)
    left, some, own, filters = pl.pallas_call(
        functools.partial(product_kernel, kinds, share, blocks, slabs),
        out_shape=[
            jax.ShapeDtypeStruct((rows, tokens), BF16),
            jax.ShapeDtypeStruct((rows, width * slabs), BF16),
            jax.ShapeDtypeStruct((rows, tokens // blocks), BF16),
            jax.ShapeDtypeStruct((share * blocks, tokens // blocks), F32),
        ],
        in_specs=[VMEM] * (blocks + 1 + slabs),
        out_specs=[VMEM] * 4,
        compiler_params=pltpu.CompilerParams(vmem_limit_bytes=VMEM_BYTES),
        cost_estimate=pl.CostEstimate(**cost),
        name="products",
    )(*grads, *turned)
    return left, some, own, filters


def last_products(left, some, turned):
    rows, known = some.shape
    tokens, width = turned.shape
    half = jax.ShapeDtypeStruct((rows // 2, known + width), BF16)
    return pl.pallas_call(
        last_kernel,
        out_shape=[half, half],
        in_specs=[VMEM] * 3,
        out_specs=[VMEM] * 2,
        compiler_params=pltpu.CompilerParams(vmem_limit_bytes=VMEM_BYTES),
        cost_estimate=pl.CostEstimate(flops=2 * rows * tokens * width, bytes_accessed=2**20, transcendentals=0),
        name="products",
    )(left, some, turned)


def piece_kernel(values_ref, out_ref):
    width = out_ref.shape[2]
    for i in range(out_ref.shape[0]):
        out_ref[i] = values_ref[:, i * width : (i + 1) * width]


def column_pieces(values, blocks):
    rows, width = values.shape
    return pl.pallas_call(
        piece_kernel,
        out_shape=jax.ShapeDtypeStruct((blocks, rows, width // blocks), values.dtype),
        in_specs=[VMEM],
        out_specs=VMEM,
        compiler_params=pltpu.CompilerParams(vmem_limit_bytes=VMEM_BYTES),
        cost_estimate=pl.CostEstimate(flops=0, bytes_accessed=2**21, transcendentals=0),
        name="pieces",
    )(values)


def input_kernel(count, *refs):
    sums = 0.0
    for grad_ref, weight_ref in zip(refs[:count], refs[count : 2 * count]):
        sums = sums + lax.dot_general(
            grad_ref[...], weight_ref[...], (((0,), (0,)), ((), ())), preferred_element_type=F32
        )
    refs[-1][...] = sums.astype(BF16)


def input_gradient(grads, weights):
    rows, length = grads[0].shape
    width = weights[0].shape[1]
    return pl.pallas_call(
        functools.partial(input_kernel, len(grads)),
        out_shape=jax.ShapeDtypeStruct((length, width), BF16),
        in_specs=[VMEM] * (2 * len(grads)),
        out_specs=VMEM,
        compiler_params=pltpu.CompilerParams(vmem_limit_bytes=VMEM_BYTES),
        cost_estimate=pl.CostEstimate(
            flops=2 * rows * len(grads) * length * width, bytes_accessed=4 * 2**20, transcendentals=0
        ),
        name="inputs",
    )(*grads, *weights)


def place_kernel(kinds, share, factor, *refs):
    out_ref = refs[-1]
    blocks = (len(refs) - 1) // 2
    place = lax.axis_index("ctx")
    slab = lax.axis_index("chan") ^ pl.program_id(0)
    width = out_ref.shape[1] // blocks
    source = pl.ds(pl.multiple_of(slab * width, width), width)
    for a in range(2):
        for r in range(blocks):
            sender = lax.rem(place + (r if a else blocks - r), blocks)
            columns = pl.ds(pl.multiple_of(sender * width, width), width)
            for b in range(2):
                for k in range(kinds):
                    row = (b * kinds + k) * share
                    value = refs[a * blocks + r][row : row + share, source].astype(F32) * factor
                    to = pl.multiple_of(k * share * blocks + (sender ^ (2 * a + b)) * share, share)
                    out_ref[pl.ds(to, share), columns] = value


def place_weights(pieces, kinds, share, slabs, factor):
    flat = [piece for group in pieces for piece in group]
    depth = flat[0].shape[1]
    rows = kinds * share * len(pieces[0])
    return pl.pallas_call(
        functools.partial(place_kernel, kinds, share, factor),
        out_shape=jax.ShapeDtypeStruct((rows, depth * slabs), F32),
        grid=(slabs,),
        in_specs=[pl.BlockSpec(flat[0].shape, lambda i: (0, 0))] * len(flat),
        out_specs=pl.BlockSpec((rows, depth), lambda i: (0, i)),
        compiler_params=pltpu.CompilerParams(vmem_limit_bytes=VMEM_BYTES),
        cost_estimate=pl.CostEstimate(flops=0, bytes_accessed=6 * 2**20, transcendentals=0),
        name="place",
    )(*flat)


def swap(values, axis, mask):
    if mask == 0:
        return values
    size = lax.axis_size(axis)
    return lax.ppermute(values, axis, [(i, i ^ mask) for i in range(size)])


def after(values, *others):
    return lax.optimization_barrier((values, *others))[0]


def gather_chan(values):
    slabs = lax.axis_size("chan")
    if slabs != 4:
        return [swap(values, "chan", m) for m in range(slabs)]
    far = swap(values, "chan", 2)
    return [values, swap(values, "chan", 1), far, swap(far, "chan", 1)]


def ring(values, step):
    size = lax.axis_size("ctx")
    found = [values]
    while len(found) < size:
        found.append(lax.ppermute(found[-1], "ctx", [(i, (i + step) % size) for i in range(size)]))
    return found


def general_tail(messages, features, place, mine, kinds, share, factor):
    blocks = lax.axis_size("ctx")
    length, width = features[0].shape
    rows = kinds * share * blocks
    grad_proj = jnp.zeros((kinds, share * blocks, length), BF16)
    grad_filter = jnp.zeros((share * blocks, length), F32)
    for m, message in enumerate(messages):
        piece = lax.dynamic_slice_in_dim(message, (place ^ m) * length, length, 1)
        piece = swap(piece, "ctx", m).reshape(kinds, share, length)
        grad_proj = lax.dynamic_update_slice_in_dim(grad_proj, piece, (place ^ m) * share, 1)
        end = swap(message[:, blocks * length :], "ctx", m).astype(F32)
        end = jnp.concatenate([end[:share], end[2 * share :, : length // 4]], axis=1)
        grad_filter = lax.dynamic_update_slice_in_dim(grad_filter, end, (place ^ m) * share, 0)
    grad_proj = grad_proj.reshape(rows, length)
    grad_weight = jnp.zeros((rows, width * len(features)), F32)
    for m, slab in enumerate(features):
        total = lax.psum(mm(grad_proj, slab).astype(BF16), "ctx").astype(F32) * factor
        grad_weight = lax.dynamic_update_slice_in_dim(grad_weight, total, (mine ^ m) * width, 1)
    return grad_proj, grad_weight, grad_filter


def per_device(activations, proj_weight, long_filter, skip_gain, out_grad):
    blocks = lax.axis_size("ctx")
    slabs = lax.axis_size("chan")
    place = lax.axis_index("ctx")
    mine = lax.axis_index("chan")
    length, width = activations.shape
    kinds, own, depth = proj_weight.shape
    share = own // blocks
    factor = (length * blocks) ** (-0.5)
    rows = kinds * own
    line = blocks == 4 and slabs == 4 and width % (blocks * LANES) == 0 and share % 16 == 0
    weight_rows = proj_weight.reshape(rows, depth)

    def share_of(array, m, axis=0, size=share):
        return lax.dynamic_slice_in_dim(array, (place ^ m) * size, size, axis)

    if line:
        features = [activations, swap(activations, "chan", 1), swap(activations, "chan", 2)]
    else:
        features = [swap(activations, "chan", m) for m in range(slabs)]

    along = [out_grad.astype(F32), long_filter]
    gain = share_of(skip_gain, 0)[None, :]

    weight_cols = [lax.dynamic_slice_in_dim(weight_rows, (mine ^ m) * width, width, 1) for m in range(slabs)]
    if line:
        turned = after(column_pieces(activations, blocks), features[1])
        turned = lax.all_to_all(turned, "ctx", split_axis=0, concat_axis=0).reshape(length * blocks, width // blocks)
        sums = project(weight_rows, [], features[:2], [0, 1])
        weight_cols[1] = swap(weight_cols[1], "chan", 1)
        features[2], sums, along, gain, weight_cols = lax.optimization_barrier(
            (features[2], sums, along, gain, weight_cols)
        )
        features.append(swap(features[2], "chan", 1))
        sums = project(weight_rows, sums, features[2:3], [2])
        pieces = project(weight_rows, sums, features[3:], [3], (blocks, kinds, along))
    else:
        sums = project(weight_rows, [], features[:1], [0])
        pieces = project(weight_rows, sums, features[1:], list(range(1, slabs)), (blocks, kinds, along))
    signals = [swap(piece, "ctx", m) for m, piece in enumerate(pieces)]
    if line:
        signals, turned = lax.optimization_barrier((signals, turned))
        turned = [turned, swap(turned, "chan", 1), swap(turned, "chan", 2)]
    messages = convolve(signals, gain)

    if line:
        messages = [messages[0], swap(messages[1], "ctx", 1), swap(messages[2], "ctx", 2), messages[3]]
        messages[3] = lax.ppermute(messages[3], "ctx", [(1, 2), (2, 1), (0, 0), (3, 3)])
        messages.append(swap(messages[2], "ctx", 1))
        far, messages = lax.optimization_barrier((turned[2], messages))
        far = swap(far, "chan", 1)
        left, some, grad_proj, grad_filter = weight_products(messages, turned, kinds, share)
        first, second = last_products(left, some, far)
        first, second, grad_proj = lax.optimization_barrier((first, second, grad_proj))
        pieces = [ring(first, 1), ring(second, -1)]
        gathered = gather_chan(grad_proj)
        weight_cols = after(weight_cols, gathered[2])
        weight_cols = [*weight_cols[:2], swap(weight_cols[2], "chan", 2), swap(weight_cols[3], "chan", 3)]
        grad_rows = input_gradient(gathered, weight_cols)
        grad_rows, pieces = lax.optimization_barrier((grad_rows, pieces))
        grad_weight = place_weights(pieces, kinds, share, slabs, factor)
    else:
        grad_proj, grad_weight, grad_filter = general_tail(messages, features, place, mine, kinds, share, factor)
        weight_cols = [swap(cols, "chan", m) for m, cols in enumerate(weight_cols)]
        grad_rows = input_gradient(gather_chan(grad_proj), weight_cols)
    return (
        grad_rows,
        grad_weight.reshape(kinds, own, depth),
        grad_filter,
    )


def solution(mesh):
    placed = (
        P(("files", "ctx"), "chan"),
        P(None, "chan", None),
        P("chan", "ctx"),
        P("chan"),
        P("chan", ("files", "ctx")),
    )
    return jax.shard_map(
        per_device,
        mesh=mesh,
        in_specs=placed,
        out_specs=(
            P(("files", "ctx"), "chan"),
            P("files", "chan", None),
            P("chan", ("files", "ctx")),
        ),
        check_vma=False,
    )
```

```python
import functools
import math

import jax
import jax.numpy as jnp
import numpy as np
from jax import lax
from jax.experimental import pallas as pl
from jax.experimental.pallas import tpu as pltpu
from jax.sharding import PartitionSpec as P

LANES = 128
BF16 = jnp.bfloat16
F32 = jnp.float32
VMEM = pl.BlockSpec(memory_space=pltpu.VMEM)
ANY = pl.BlockSpec(memory_space=pl.ANY)
VMEM_BYTES = 16 * 2**20


def split_table(table):
    high = np.asarray(table, np.float32).astype(BF16)
    low = (np.asarray(table, np.float64) - high.astype(np.float64)).astype(BF16)
    return np.stack([high, low])


def fourier_tables(tokens, group):
    period = 2 * tokens
    rows = period // LANES
    used = rows // 2
    freqs = rows // 2 + 1
    part = -(-freqs * group // 8) * 8
    k1 = np.arange(freqs)
    n1 = np.arange(used)
    angle = 2.0 * math.pi * (np.outer(k1, n1) % rows) / rows
    eye = np.eye(group)
    forward = np.zeros((2 * part, used * group))
    forward[: freqs * group] = np.kron(np.cos(angle), eye)
    forward[part : part + freqs * group] = np.kron(-np.sin(angle), eye)
    weight = np.where((k1 == 0) | (k1 == rows // 2), 1.0, 2.0)[None, :] / period
    inverse = np.zeros((used * group, 2 * part))
    inverse[:, : freqs * group] = np.kron(np.cos(angle.T) * weight, eye)
    inverse[:, part : part + freqs * group] = np.kron(-np.sin(angle.T) * weight, eye)
    n2 = np.arange(LANES)
    turn = 2.0 * math.pi * np.outer(k1, n2) / period
    twiddle = np.zeros((2, part, LANES), np.float32)
    twiddle[0, : freqs * group] = np.repeat(np.cos(turn), group, axis=0)
    twiddle[1, : freqs * group] = np.repeat(np.sin(turn), group, axis=0)
    inner = 2.0 * math.pi * (np.outer(n2, n2) % LANES) / LANES
    cos, sin = np.cos(inner), np.sin(inner)
    second = np.block([[cos, -sin], [sin, cos]])
    second_back = np.block([[cos, sin], [-sin, cos]])
    return (
        split_table(forward),
        split_table(second),
        split_table(second_back),
        split_table(inverse),
        twiddle,
    )


def halves(values):
    high = values.astype(BF16)
    return high, (values - high.astype(F32)).astype(BF16)


def mm(left, right):
    return jnp.dot(left, right, preferred_element_type=F32)


def table_left(table, values):
    high, low = halves(values)
    return mm(table[0], high) + (mm(table[0], low) + mm(table[1], high))


def table_right(values, table):
    high, low = halves(values)
    return mm(high, table[0]) + (mm(low, table[0]) + mm(high, table[1]))


def conv_kernel(blocks, chans, group, factor, *refs):
    count = blocks + 5
    gain_ref, sources, refs = refs[0], refs[1 : 1 + count], refs[1 + count :]
    out_refs = refs[:blocks]
    series, results, inputs = refs[blocks : 3 + blocks]
    held = refs[3 + blocks : 3 + blocks + count]
    sems = refs[3 + blocks + count]
    copies = [pltpu.make_async_copy(sources[i], held[i], sems.at[i]) for i in range(count)]
    for copy in copies:
        copy.start()
    signal_refs = held[:blocks]
    fwd_ref, second_ref, back_ref, inv_ref, twiddle_ref = held[blocks:]
    place = lax.axis_index("ctx")
    length = series.shape[-1]
    cuts = length // LANES
    for m in range(blocks):
        where = place ^ m
        copies[m].wait()
        values = signal_refs[m][...].astype(F32)
        upstream = values[3 * chans : 4 * chans]
        inputs[0, where] = values[:chans]
        inputs[1, where] = values[2 * chans : 3 * chans]
        inputs[2, where] = upstream
        series[0, where] = values[4 * chans :] * factor
        series[1, where] = values[:chans] * values[2 * chans : 3 * chans]
        series[2, where] = upstream * values[chans : 2 * chans]
    for copy in copies[blocks:]:
        copy.wait()
    part = twiddle_ref.shape[1]
    cos, sin = twiddle_ref[0], twiddle_ref[1]
    for start in range(0, chans, group):
        picked = []
        for q in range(3):
            tiles = []
            for z in range(blocks):
                loaded = series[q, z]
                loaded = loaded[start : start + group]
                for n in range(cuts):
                    tiles.append(loaded[:, n * LANES : (n + 1) * LANES])
            picked.append(jnp.concatenate(tiles, axis=0))
        first = table_left(fwd_ref, jnp.concatenate(picked, axis=1))
        turned = []
        for q in range(3):
            re = first[:part, q * LANES : (q + 1) * LANES]
            im = first[part:, q * LANES : (q + 1) * LANES]
            turned.append(jnp.concatenate([re * cos + im * sin, im * cos - re * sin], axis=1))
        spectra = table_right(jnp.concatenate(turned, axis=0), second_ref)
        parts = [
            (spectra[q * part : (q + 1) * part, :LANES], spectra[q * part : (q + 1) * part, LANES:])
            for q in range(3)
        ]
        (fr, fi), (gr, gi), (ur, ui) = parts
        products = jnp.concatenate(
            [
                jnp.concatenate([fr * gr - fi * gi, fr * gi + fi * gr], axis=1),
                jnp.concatenate([fr * ur + fi * ui, fr * ui - fi * ur], axis=1),
                jnp.concatenate([gr * ur + gi * ui, gr * ui - gi * ur], axis=1),
            ],
            axis=0,
        )
        back = table_right(products, back_ref)
        turned = []
        for q in range(3):
            re = back[q * part : (q + 1) * part, :LANES]
            im = back[q * part : (q + 1) * part, LANES:]
            turned.append(jnp.concatenate([re * cos - im * sin, im * cos + re * sin], axis=0))
        final = table_left(inv_ref, jnp.concatenate(turned, axis=1))
        for q in range(3):
            for z in range(blocks):
                tiles = [
                    final[(z * cuts + n) * group : (z * cuts + n + 1) * group, q * LANES : (q + 1) * LANES]
                    for n in range(cuts)
                ]
                results[q, z, start : start + group, :] = jnp.concatenate(tiles, axis=1)
    down = lax.broadcasted_iota(jnp.int32, (chans, chans), 0)
    along = lax.broadcasted_iota(jnp.int32, (chans, chans), 1)
    gain = jnp.sum(jnp.where(down == along, gain_ref[...], 0.0), axis=1, keepdims=True)
    for z in range(blocks):
        conv_out = results[0, z] + gain * series[1, z]
        grad_gated = results[1, z] + gain * series[2, z]
        grads = jnp.concatenate(
            [grad_gated * inputs[1, z], inputs[2, z] * conv_out, grad_gated * inputs[0, z]], axis=0
        ).astype(BF16)
        for ref in out_refs:
            ref[:, z * length : (z + 1) * length] = grads
    found = [(factor * results[2, place ^ m]).astype(BF16).astype(F32) for m in range(blocks)]
    cut = 3 * length // 4
    rest = jnp.zeros((chans, length - cut), F32)
    for m in range(blocks):
        pair = found[m], found[min(m ^ 1, blocks - 1)]
        last = jnp.concatenate([pair[0][:, cut:], pair[1][:, cut:], rest], axis=1)
        rows = jnp.concatenate([pair[0][:, :cut], pair[1][:, :cut], last], axis=0)
        out_refs[m][:, blocks * length :] = rows.astype(BF16)


def convolve(signals, gain):
    blocks = len(signals)
    chans, length = signals[0].shape[0] // 5, signals[0].shape[1]
    tokens = blocks * length
    group = max(1, min(chans, 8, LANES * LANES // tokens))
    tables = fourier_tables(tokens, group)
    arrays = [*signals, *[jnp.asarray(table) for table in tables]]
    part = tables[4].shape[1]
    flops = 2 * 3 * (chans // group) * 3 * (4 * part * group * (tokens // LANES) * LANES + 2 * part * 256 * 256)
    return pl.pallas_call(
        functools.partial(conv_kernel, blocks, chans, group, tokens ** (-0.5)),
        out_shape=[jax.ShapeDtypeStruct((3 * chans, tokens + 3 * length // 4), BF16)] * blocks,
        in_specs=[VMEM] + [ANY] * len(arrays),
        out_specs=[VMEM] * blocks,
        scratch_shapes=[pltpu.VMEM((3, blocks, chans, length), F32)] * 3
        + [pltpu.VMEM(array.shape, array.dtype) for array in arrays]
        + [pltpu.SemaphoreType.DMA((len(arrays),))],
        compiler_params=pltpu.CompilerParams(vmem_limit_bytes=60 * 2**20),
        cost_estimate=pl.CostEstimate(flops=flops, bytes_accessed=4 * 2**20, transcendentals=0),
        name="conv",
    )(gain, *arrays)


def partial_rows(weight_ref, refs, masks):
    mine = lax.axis_index("chan")
    sums = 0.0
    for m, ref in zip(masks, refs):
        width = ref.shape[1]
        at = pl.multiple_of((mine ^ m) * width, width)
        sums = sums + lax.dot_general(
            ref[...], weight_ref[:, pl.ds(at, width)], (((1,), (1,)), ((), ())), preferred_element_type=F32
        )
    return sums


def start_kernel(masks, weight_ref, *refs):
    refs[-1][...] = partial_rows(weight_ref, refs[:-1], masks)


def more_kernel(masks, weight_ref, sum_ref, *refs):
    refs[-1][...] = sum_ref[...] + partial_rows(weight_ref, refs[:-1], masks)


def finish_kernel(masks, blocks, kinds, share, given_ref, filter_ref, weight_ref, sum_ref, *refs):
    out_refs = refs[len(masks) : len(masks) + blocks]
    total = refs[-1]
    place = lax.axis_index("ctx")
    total[...] = (sum_ref[...] + partial_rows(weight_ref, refs[: len(masks)], masks)).T
    for m in range(blocks):
        first = (place ^ m) * share
        rows = [total[pl.ds(pl.multiple_of(k * share * blocks + first, share), share), :] for k in range(kinds)]
        for ref in (given_ref, filter_ref):
            rows.append(ref[pl.ds(pl.multiple_of(first, share), share), :])
        out_refs[m][...] = jnp.concatenate(rows, axis=0).astype(BF16)


def project(weight_rows, sums, features, masks, out=None):
    rows, depth = weight_rows.shape
    length, width = features[0].shape
    along = []
    if out is None:
        body = functools.partial(more_kernel if sums else start_kernel, masks)
        shape = [jax.ShapeDtypeStruct((length, rows), F32)]
    else:
        blocks, kinds, along = out
        share = rows // kinds // blocks
        body = functools.partial(finish_kernel, masks, blocks, kinds, share)
        shape = [jax.ShapeDtypeStruct(((kinds + 2) * share, length), BF16)] * blocks
    flops = 2 * rows * length * width * len(masks)
    return pl.pallas_call(
        body,
        out_shape=shape,
        in_specs=[VMEM] * (len(along) + 1 + len(sums) + len(features)),
        out_specs=[VMEM] * len(shape),
        scratch_shapes=[pltpu.VMEM((rows, length), F32)] if out else [],
        compiler_params=pltpu.CompilerParams(vmem_limit_bytes=VMEM_BYTES),
        cost_estimate=pl.CostEstimate(flops=flops, bytes_accessed=2**20, transcendentals=0),
        name="project",
    )(*along, weight_rows, *sums, *features)


def product_kernel(kinds, share, blocks, slabs, *refs):
    grad_refs, turned = refs[: blocks + 1], refs[blocks + 1 : blocks + 1 + slabs]
    left_ref, some_ref, own_ref, filter_ref = refs[blocks + 1 + slabs :]
    place = lax.axis_index("ctx")
    length = own_ref.shape[1]
    width = turned[0].shape[1]
    rows = kinds * share
    tokens = blocks * length
    mine = pl.ds(pl.multiple_of(place * length, length), length)
    middle = (place == 1) | (place == 2)
    for m in range(blocks):
        value = grad_refs[m][:, :tokens]
        if m == blocks - 1:
            value = jnp.where(middle, value, grad_refs[blocks][:, :tokens])
        left_ref[m * rows : (m + 1) * rows, :] = value
        for k in range(kinds):
            to = pl.multiple_of(k * share * blocks + (place ^ m) * share, share)
            own_ref[pl.ds(to, share), :] = left_ref[m * rows + k * share : m * rows + (k + 1) * share, mine]
        end = grad_refs[m][:, tokens:].astype(F32)
        cut = end.shape[1]
        size = length - cut
        given = jnp.concatenate([end[:share], end[2 * share :, :size]], axis=1)
        if m == blocks - 1:
            end = grad_refs[blocks][:, tokens:].astype(F32)
            handed = jnp.concatenate([end[share : 2 * share], end[2 * share :, size : 2 * size]], axis=1)
            given = jnp.where(middle, given, handed)
        to = pl.multiple_of((place ^ m) * share, share)
        filter_ref[pl.ds(to, share), :] = given
    for i in range(slabs):
        some_ref[:, i * width : (i + 1) * width] = mm(left_ref[...], turned[i][...]).astype(BF16)


def last_kernel(left_ref, some_ref, turned_ref, first_ref, second_ref):
    half, known = first_ref.shape[0], some_ref.shape[1]
    value = mm(left_ref[...], turned_ref[...]).astype(BF16)
    for i, ref in enumerate((first_ref, second_ref)):
        ref[:, :known] = some_ref[i * half : (i + 1) * half, :]
        ref[:, known:] = value[i * half : (i + 1) * half]


def weight_products(grads, turned, kinds, share):
    blocks, slabs = len(grads) - 1, len(turned)
    tokens, width = turned[0].shape
    rows = kinds * share * blocks
    cost = dict(flops=2 * rows * tokens * width * slabs, bytes_accessed=4 * 2**20, transcendentals=0)
    left, some, own, filters = pl.pallas_call(
        functools.partial(product_kernel, kinds, share, blocks, slabs),
        out_shape=[
            jax.ShapeDtypeStruct((rows, tokens), BF16),
            jax.ShapeDtypeStruct((rows, width * slabs), BF16),
            jax.ShapeDtypeStruct((rows, tokens // blocks), BF16),
            jax.ShapeDtypeStruct((share * blocks, tokens // blocks), F32),
        ],
        in_specs=[VMEM] * (blocks + 1 + slabs),
        out_specs=[VMEM] * 4,
        compiler_params=pltpu.CompilerParams(vmem_limit_bytes=VMEM_BYTES),
        cost_estimate=pl.CostEstimate(**cost),
        name="products",
    )(*grads, *turned)
    return left, some, own, filters


def last_products(left, some, turned):
    rows, known = some.shape
    tokens, width = turned.shape
    half = jax.ShapeDtypeStruct((rows // 2, known + width), BF16)
    return pl.pallas_call(
        last_kernel,
        out_shape=[half, half],
        in_specs=[VMEM] * 3,
        out_specs=[VMEM] * 2,
        compiler_params=pltpu.CompilerParams(vmem_limit_bytes=VMEM_BYTES),
        cost_estimate=pl.CostEstimate(flops=2 * rows * tokens * width, bytes_accessed=2**20, transcendentals=0),
        name="products",
    )(left, some, turned)


def piece_kernel(values_ref, out_ref):
    width = out_ref.shape[2]
    for i in range(out_ref.shape[0]):
        out_ref[i] = values_ref[:, i * width : (i + 1) * width]


def column_pieces(values, blocks):
    rows, width = values.shape
    return pl.pallas_call(
        piece_kernel,
        out_shape=jax.ShapeDtypeStruct((blocks, rows, width // blocks), values.dtype),
        in_specs=[VMEM],
        out_specs=VMEM,
        compiler_params=pltpu.CompilerParams(vmem_limit_bytes=VMEM_BYTES),
        cost_estimate=pl.CostEstimate(flops=0, bytes_accessed=2**21, transcendentals=0),
        name="pieces",
    )(values)


def input_kernel(count, *refs):
    sums = 0.0
    for grad_ref, weight_ref in zip(refs[:count], refs[count : 2 * count]):
        sums = sums + lax.dot_general(
            grad_ref[...], weight_ref[...], (((0,), (0,)), ((), ())), preferred_element_type=F32
        )
    refs[-1][...] = sums.astype(BF16)


def input_gradient(grads, weights):
    rows, length = grads[0].shape
    width = weights[0].shape[1]
    return pl.pallas_call(
        functools.partial(input_kernel, len(grads)),
        out_shape=jax.ShapeDtypeStruct((length, width), BF16),
        in_specs=[VMEM] * (2 * len(grads)),
        out_specs=VMEM,
        compiler_params=pltpu.CompilerParams(vmem_limit_bytes=VMEM_BYTES),
        cost_estimate=pl.CostEstimate(
            flops=2 * rows * len(grads) * length * width, bytes_accessed=4 * 2**20, transcendentals=0
        ),
        name="inputs",
    )(*grads, *weights)


def place_kernel(kinds, share, factor, *refs):
    out_ref = refs[-1]
    some = (len(refs) - 1) // 2
    blocks = some + 1
    place = lax.axis_index("ctx")
    slab = lax.axis_index("chan") ^ pl.program_id(0)
    width = out_ref.shape[1] // blocks
    source = pl.ds(pl.multiple_of(slab * width, width), width)
    for i, ref in enumerate(refs[:-1]):
        a, r = divmod(i, some)
        sender = lax.rem(place + (r if a else blocks - r), blocks)
        columns = pl.ds(pl.multiple_of(sender * width, width), width)
        for b in range(2):
            for k in range(kinds):
                row = (b * kinds + k) * share
                value = ref[row : row + share, source].astype(F32) * factor
                to = pl.multiple_of(k * share * blocks + (sender ^ (2 * a + b)) * share, share)
                out_ref[pl.ds(to, share), columns] = value


def place_last_kernel(kinds, share, blocks, slabs, factor, *refs):
    out_ref, held, sems = refs[-3:]
    place = lax.axis_index("ctx")
    mine = lax.axis_index("chan")
    width = refs[0].shape[1] // slabs
    copies = []
    for a in range(2):
        sender = lax.rem(place + (blocks - 1 if a else 1), blocks)
        base = (sender ^ (2 * a)) // 2 * 2 * share
        for k in range(kinds):
            for b in range(2):
                row = (b * kinds + k) * share
                to = pl.multiple_of((2 * k + lax.rem(sender + b, 2)) * share, share)
                held[a, pl.ds(to, share), :] = refs[a][row : row + share, :].astype(F32) * factor
            rows = pl.ds(pl.multiple_of(k * share * blocks + base, 2 * share), 2 * share)
            for i in range(slabs):
                columns = pl.ds(pl.multiple_of(((mine ^ i) * blocks + sender) * width, width), width)
                source = held.at[a, 2 * k * share : 2 * (k + 1) * share, i * width : (i + 1) * width]
                copies.append(pltpu.make_async_copy(source, out_ref.at[rows, columns], sems.at[len(copies)]))
                copies[-1].start()
    for copy in copies:
        copy.wait()


def place_weights(pieces, kinds, share, slabs, factor):
    flat = [piece for group in pieces for piece in group[:-1]]
    last = [group[-1] for group in pieces]
    blocks, depth = len(pieces[0]), flat[0].shape[1]
    rows = kinds * share * blocks
    shape = jax.ShapeDtypeStruct((rows, depth * slabs), F32)
    most = pl.pallas_call(
        functools.partial(place_kernel, kinds, share, factor),
        out_shape=shape,
        grid=(slabs,),
        in_specs=[pl.BlockSpec(flat[0].shape, lambda i: (0, 0))] * len(flat),
        out_specs=pl.BlockSpec((rows, depth), lambda i: (0, i)),
        compiler_params=pltpu.CompilerParams(vmem_limit_bytes=VMEM_BYTES),
        cost_estimate=pl.CostEstimate(flops=0, bytes_accessed=6 * 2**20, transcendentals=0),
        name="place",
    )(*flat)
    return pl.pallas_call(
        functools.partial(place_last_kernel, kinds, share, blocks, slabs, factor),
        out_shape=shape,
        in_specs=[VMEM, VMEM, ANY],
        out_specs=ANY,
        scratch_shapes=[
            pltpu.VMEM((2, 2 * kinds * share, depth), F32),
            pltpu.SemaphoreType.DMA((2 * kinds * slabs,)),
        ],
        input_output_aliases={2: 0},
        compiler_params=pltpu.CompilerParams(vmem_limit_bytes=VMEM_BYTES),
        cost_estimate=pl.CostEstimate(flops=0, bytes_accessed=2**20, transcendentals=0),
        name="place",
    )(*last, most)


def swap(values, axis, mask):
    if mask == 0:
        return values
    size = lax.axis_size(axis)
    return lax.ppermute(values, axis, [(i, i ^ mask) for i in range(size)])


def after(values, *others):
    return lax.optimization_barrier((values, *others))[0]


def gather_chan(values):
    slabs = lax.axis_size("chan")
    if slabs != 4:
        return [swap(values, "chan", m) for m in range(slabs)]
    far = swap(values, "chan", 2)
    return [values, swap(values, "chan", 1), far, swap(far, "chan", 1)]


def ring(values, step):
    size = lax.axis_size("ctx")
    found = [values]
    while len(found) < size:
        found.append(lax.ppermute(found[-1], "ctx", [(i, (i + step) % size) for i in range(size)]))
    return found


def general_tail(messages, features, place, mine, kinds, share, factor):
    blocks = lax.axis_size("ctx")
    length, width = features[0].shape
    rows = kinds * share * blocks
    grad_proj = jnp.zeros((kinds, share * blocks, length), BF16)
    grad_filter = jnp.zeros((share * blocks, length), F32)
    for m, message in enumerate(messages):
        piece = lax.dynamic_slice_in_dim(message, (place ^ m) * length, length, 1)
        piece = swap(piece, "ctx", m).reshape(kinds, share, length)
        grad_proj = lax.dynamic_update_slice_in_dim(grad_proj, piece, (place ^ m) * share, 1)
        end = swap(message[:, blocks * length :], "ctx", m).astype(F32)
        end = jnp.concatenate([end[:share], end[2 * share :, : length // 4]], axis=1)
        grad_filter = lax.dynamic_update_slice_in_dim(grad_filter, end, (place ^ m) * share, 0)
    grad_proj = grad_proj.reshape(rows, length)
    grad_weight = jnp.zeros((rows, width * len(features)), F32)
    for m, slab in enumerate(features):
        total = lax.psum(mm(grad_proj, slab).astype(BF16), "ctx").astype(F32) * factor
        grad_weight = lax.dynamic_update_slice_in_dim(grad_weight, total, (mine ^ m) * width, 1)
    return grad_proj, grad_weight, grad_filter


def per_device(activations, proj_weight, long_filter, skip_gain, out_grad):
    blocks = lax.axis_size("ctx")
    slabs = lax.axis_size("chan")
    place = lax.axis_index("ctx")
    mine = lax.axis_index("chan")
    length, width = activations.shape
    kinds, own, depth = proj_weight.shape
    share = own // blocks
    factor = (length * blocks) ** (-0.5)
    rows = kinds * own
    line = blocks == 4 and slabs == 4 and width % (blocks * LANES) == 0 and share % 16 == 0
    weight_rows = proj_weight.reshape(rows, depth)

    def share_of(array, m, axis=0, size=share):
        return lax.dynamic_slice_in_dim(array, (place ^ m) * size, size, axis)

    if line:
        features = [activations, swap(activations, "chan", 1), swap(activations, "chan", 2)]
    else:
        features = [swap(activations, "chan", m) for m in range(slabs)]

    along = [out_grad.astype(F32), long_filter]
    gain = share_of(skip_gain, 0)[None, :]

    weight_cols = [lax.dynamic_slice_in_dim(weight_rows, (mine ^ m) * width, width, 1) for m in range(slabs)]
    if line:
        turned = after(column_pieces(activations, blocks), features[1])
        turned = lax.all_to_all(turned, "ctx", split_axis=0, concat_axis=0).reshape(length * blocks, width // blocks)
        sums = project(weight_rows, [], features[:2], [0, 1])
        weight_cols[1] = swap(weight_cols[1], "chan", 1)
        features[2], sums, along, gain, weight_cols = lax.optimization_barrier(
            (features[2], sums, along, gain, weight_cols)
        )
        features.append(swap(features[2], "chan", 1))
        sums = project(weight_rows, sums, features[2:3], [2])
        pieces = project(weight_rows, sums, features[3:], [3], (blocks, kinds, along))
    else:
        sums = project(weight_rows, [], features[:1], [0])
        pieces = project(weight_rows, sums, features[1:], list(range(1, slabs)), (blocks, kinds, along))
    signals = [swap(piece, "ctx", m) for m, piece in enumerate(pieces)]
    if line:
        signals, turned = lax.optimization_barrier((signals, turned))
        turned = [turned, swap(turned, "chan", 1), swap(turned, "chan", 2)]
    messages = convolve(signals, gain)

    if line:
        messages = [messages[0], swap(messages[1], "ctx", 1), swap(messages[2], "ctx", 2), messages[3]]
        messages[3] = lax.ppermute(messages[3], "ctx", [(1, 2), (2, 1), (0, 0), (3, 3)])
        messages.append(swap(messages[2], "ctx", 1))
        far, messages = lax.optimization_barrier((turned[2], messages))
        far = swap(far, "chan", 1)
        left, some, grad_proj, grad_filter = weight_products(messages, turned, kinds, share)
        first, second = last_products(left, some, far)
        first, second, grad_proj = lax.optimization_barrier((first, second, grad_proj))
        pieces = [ring(first, 1), ring(second, -1)]
        gathered = gather_chan(grad_proj)
        weight_cols = after(weight_cols, gathered[2])
        weight_cols = [*weight_cols[:2], swap(weight_cols[2], "chan", 2), swap(weight_cols[3], "chan", 3)]
        grad_rows = input_gradient(gathered, weight_cols)
        grad_rows, pieces[0][-1], pieces[1][-1] = lax.optimization_barrier(
            (grad_rows, pieces[0][-1], pieces[1][-1])
        )
        grad_weight = place_weights(pieces, kinds, share, slabs, factor)
    else:
        grad_proj, grad_weight, grad_filter = general_tail(messages, features, place, mine, kinds, share, factor)
        weight_cols = [swap(cols, "chan", m) for m, cols in enumerate(weight_cols)]
        grad_rows = input_gradient(gather_chan(grad_proj), weight_cols)
    return (
        grad_rows,
        grad_weight.reshape(kinds, own, depth),
        grad_filter,
    )


def solution(mesh):
    placed = (
        P(("files", "ctx"), "chan"),
        P(None, "chan", None),
        P("chan", "ctx"),
        P("chan"),
        P("chan", ("files", "ctx")),
    )
    return jax.shard_map(
        per_device,
        mesh=mesh,
        in_specs=placed,
        out_specs=(
            P(("files", "ctx"), "chan"),
            P("files", "chan", None),
            P("chan", ("files", "ctx")),
        ),
        check_vma=False,
    )
```

```python
import functools
import math

import jax
import jax.numpy as jnp
import numpy as np
from jax import lax
from jax.experimental import pallas as pl
from jax.experimental.pallas import tpu as pltpu
from jax.sharding import PartitionSpec as P

LANES = 128
BF16 = jnp.bfloat16
F32 = jnp.float32
VMEM = pl.BlockSpec(memory_space=pltpu.VMEM)
ANY = pl.BlockSpec(memory_space=pl.ANY)
VMEM_BYTES = 16 * 2**20


def split_table(table):
    high = np.asarray(table, np.float32).astype(BF16)
    low = (np.asarray(table, np.float64) - high.astype(np.float64)).astype(BF16)
    return np.stack([high, low])


def fourier_tables(tokens, group):
    period = 2 * tokens
    rows = period // LANES
    used = rows // 2
    freqs = rows // 2 + 1
    part = -(-freqs * group // 8) * 8
    k1 = np.arange(freqs)
    n1 = np.arange(used)
    angle = 2.0 * math.pi * (np.outer(k1, n1) % rows) / rows
    eye = np.eye(group)
    forward = np.zeros((2 * part, used * group))
    forward[: freqs * group] = np.kron(np.cos(angle), eye)
    forward[part : part + freqs * group] = np.kron(-np.sin(angle), eye)
    weight = np.where((k1 == 0) | (k1 == rows // 2), 1.0, 2.0)[None, :] / period
    inverse = np.zeros((used * group, 2 * part))
    inverse[:, : freqs * group] = np.kron(np.cos(angle.T) * weight, eye)
    inverse[:, part : part + freqs * group] = np.kron(-np.sin(angle.T) * weight, eye)
    n2 = np.arange(LANES)
    turn = 2.0 * math.pi * np.outer(k1, n2) / period
    twiddle = np.zeros((2, part, LANES), np.float32)
    twiddle[0, : freqs * group] = np.repeat(np.cos(turn), group, axis=0)
    twiddle[1, : freqs * group] = np.repeat(np.sin(turn), group, axis=0)
    inner = 2.0 * math.pi * (np.outer(n2, n2) % LANES) / LANES
    cos, sin = np.cos(inner), np.sin(inner)
    second = np.block([[cos, -sin], [sin, cos]])
    second_back = np.block([[cos, sin], [-sin, cos]])
    return (
        split_table(forward),
        split_table(second),
        split_table(second_back),
        split_table(inverse),
        twiddle,
    )


def halves(values):
    high = values.astype(BF16)
    return high, (values - high.astype(F32)).astype(BF16)


def mm(left, right):
    return jnp.dot(left, right, preferred_element_type=F32)


def table_left(table, values):
    high, low = halves(values)
    return mm(table[0], high) + (mm(table[0], low) + mm(table[1], high))


def table_right(values, table):
    high, low = halves(values)
    return mm(high, table[0]) + (mm(low, table[0]) + mm(high, table[1]))


def conv_kernel(blocks, chans, group, factor, *refs):
    count = blocks + 5
    gain_ref, sources, refs = refs[0], refs[1 : 1 + count], refs[1 + count :]
    out_refs = refs[:blocks]
    series, results, inputs = refs[blocks : 3 + blocks]
    held = refs[3 + blocks : 3 + blocks + count]
    sems = refs[3 + blocks + count]
    copies = [pltpu.make_async_copy(sources[i], held[i], sems.at[i]) for i in range(count)]
    for copy in copies:
        copy.start()
    signal_refs = held[:blocks]
    fwd_ref, second_ref, back_ref, inv_ref, twiddle_ref = held[blocks:]
    place = lax.axis_index("ctx")
    length = series.shape[-1]
    cuts = length // LANES
    for m in range(blocks):
        where = place ^ m
        copies[m].wait()
        values = signal_refs[m][...].astype(F32)
        upstream = values[3 * chans : 4 * chans]
        inputs[0, where] = values[:chans]
        inputs[1, where] = values[2 * chans : 3 * chans]
        inputs[2, where] = upstream
        series[0, where] = values[4 * chans :] * factor
        series[1, where] = values[:chans] * values[2 * chans : 3 * chans]
        series[2, where] = upstream * values[chans : 2 * chans]
    for copy in copies[blocks:]:
        copy.wait()
    part = twiddle_ref.shape[1]
    cos, sin = twiddle_ref[0], twiddle_ref[1]
    for start in range(0, chans, group):
        picked = []
        for q in range(3):
            tiles = []
            for z in range(blocks):
                loaded = series[q, z]
                loaded = loaded[start : start + group]
                for n in range(cuts):
                    tiles.append(loaded[:, n * LANES : (n + 1) * LANES])
            picked.append(jnp.concatenate(tiles, axis=0))
        first = table_left(fwd_ref, jnp.concatenate(picked, axis=1))
        turned = []
        for q in range(3):
            re = first[:part, q * LANES : (q + 1) * LANES]
            im = first[part:, q * LANES : (q + 1) * LANES]
            turned.append(jnp.concatenate([re * cos + im * sin, im * cos - re * sin], axis=1))
        spectra = table_right(jnp.concatenate(turned, axis=0), second_ref)
        parts = [
            (spectra[q * part : (q + 1) * part, :LANES], spectra[q * part : (q + 1) * part, LANES:])
            for q in range(3)
        ]
        (fr, fi), (gr, gi), (ur, ui) = parts
        products = jnp.concatenate(
            [
                jnp.concatenate([fr * gr - fi * gi, fr * gi + fi * gr], axis=1),
                jnp.concatenate([fr * ur + fi * ui, fr * ui - fi * ur], axis=1),
                jnp.concatenate([gr * ur + gi * ui, gr * ui - gi * ur], axis=1),
            ],
            axis=0,
        )
        back = table_right(products, back_ref)
        turned = []
        for q in range(3):
            re = back[q * part : (q + 1) * part, :LANES]
            im = back[q * part : (q + 1) * part, LANES:]
            turned.append(jnp.concatenate([re * cos - im * sin, im * cos + re * sin], axis=0))
        final = table_left(inv_ref, jnp.concatenate(turned, axis=1))
        for q in range(3):
            for z in range(blocks):
                tiles = [
                    final[(z * cuts + n) * group : (z * cuts + n + 1) * group, q * LANES : (q + 1) * LANES]
                    for n in range(cuts)
                ]
                results[q, z, start : start + group, :] = jnp.concatenate(tiles, axis=1)
    down = lax.broadcasted_iota(jnp.int32, (chans, chans), 0)
    along = lax.broadcasted_iota(jnp.int32, (chans, chans), 1)
    gain = jnp.sum(jnp.where(down == along, gain_ref[...], 0.0), axis=1, keepdims=True)
    for z in range(blocks):
        conv_out = results[0, z] + gain * series[1, z]
        grad_gated = results[1, z] + gain * series[2, z]
        grads = jnp.concatenate(
            [grad_gated * inputs[1, z], inputs[2, z] * conv_out, grad_gated * inputs[0, z]], axis=0
        ).astype(BF16)
        for ref in out_refs:
            ref[:, z * length : (z + 1) * length] = grads
    found = [(factor * results[2, place ^ m]).astype(BF16).astype(F32) for m in range(blocks)]
    cut = 3 * length // 4
    rest = jnp.zeros((chans, length - cut), F32)
    for m in range(blocks):
        pair = found[m], found[min(m ^ 1, blocks - 1)]
        last = jnp.concatenate([pair[0][:, cut:], pair[1][:, cut:], rest], axis=1)
        rows = jnp.concatenate([pair[0][:, :cut], pair[1][:, :cut], last], axis=0)
        out_refs[m][:, blocks * length :] = rows.astype(BF16)


def convolve(signals, gain):
    blocks = len(signals)
    chans, length = signals[0].shape[0] // 5, signals[0].shape[1]
    tokens = blocks * length
    group = max(1, min(chans, 8, LANES * LANES // tokens))
    tables = fourier_tables(tokens, group)
    arrays = [*signals, *[jnp.asarray(table) for table in tables]]
    part = tables[4].shape[1]
    flops = 2 * 3 * (chans // group) * 3 * (4 * part * group * (tokens // LANES) * LANES + 2 * part * 256 * 256)
    return pl.pallas_call(
        functools.partial(conv_kernel, blocks, chans, group, tokens ** (-0.5)),
        out_shape=[jax.ShapeDtypeStruct((3 * chans, tokens + 3 * length // 4), BF16)] * blocks,
        in_specs=[VMEM] + [ANY] * len(arrays),
        out_specs=[VMEM] * blocks,
        scratch_shapes=[pltpu.VMEM((3, blocks, chans, length), F32)] * 3
        + [pltpu.VMEM(array.shape, array.dtype) for array in arrays]
        + [pltpu.SemaphoreType.DMA((len(arrays),))],
        compiler_params=pltpu.CompilerParams(vmem_limit_bytes=60 * 2**20),
        cost_estimate=pl.CostEstimate(flops=flops, bytes_accessed=4 * 2**20, transcendentals=0),
        name="conv",
    )(gain, *arrays)


def partial_rows(weight_ref, refs, masks):
    mine = lax.axis_index("chan")
    sums = 0.0
    for m, ref in zip(masks, refs):
        width = ref.shape[1]
        at = pl.multiple_of((mine ^ m) * width, width)
        sums = sums + lax.dot_general(
            ref[...], weight_ref[:, pl.ds(at, width)], (((1,), (1,)), ((), ())), preferred_element_type=F32
        )
    return sums


def start_kernel(masks, weight_ref, *refs):
    refs[-1][...] = partial_rows(weight_ref, refs[:-1], masks)


def more_kernel(masks, weight_ref, sum_ref, *refs):
    refs[-1][...] = sum_ref[...] + partial_rows(weight_ref, refs[:-1], masks)


def finish_kernel(masks, blocks, kinds, share, given_ref, filter_ref, weight_ref, sum_ref, *refs):
    out_refs = refs[len(masks) : len(masks) + blocks]
    total = refs[-1]
    place = lax.axis_index("ctx")
    total[...] = (sum_ref[...] + partial_rows(weight_ref, refs[: len(masks)], masks)).T
    for m in range(blocks):
        first = (place ^ m) * share
        rows = [total[pl.ds(pl.multiple_of(k * share * blocks + first, share), share), :] for k in range(kinds)]
        for ref in (given_ref, filter_ref):
            rows.append(ref[pl.ds(pl.multiple_of(first, share), share), :])
        out_refs[m][...] = jnp.concatenate(rows, axis=0).astype(BF16)


def project(weight_rows, sums, features, masks, out=None):
    rows, depth = weight_rows.shape
    length, width = features[0].shape
    along = []
    if out is None:
        body = functools.partial(more_kernel if sums else start_kernel, masks)
        shape = [jax.ShapeDtypeStruct((length, rows), F32)]
    else:
        blocks, kinds, along = out
        share = rows // kinds // blocks
        body = functools.partial(finish_kernel, masks, blocks, kinds, share)
        shape = [jax.ShapeDtypeStruct(((kinds + 2) * share, length), BF16)] * blocks
    flops = 2 * rows * length * width * len(masks)
    return pl.pallas_call(
        body,
        out_shape=shape,
        in_specs=[VMEM] * (len(along) + 1 + len(sums) + len(features)),
        out_specs=[VMEM] * len(shape),
        scratch_shapes=[pltpu.VMEM((rows, length), F32)] if out else [],
        compiler_params=pltpu.CompilerParams(vmem_limit_bytes=VMEM_BYTES),
        cost_estimate=pl.CostEstimate(flops=flops, bytes_accessed=2**20, transcendentals=0),
        name="project",
    )(*along, weight_rows, *sums, *features)


def product_kernel(kinds, share, blocks, slabs, *refs):
    grad_refs, turned = refs[: blocks + 1], refs[blocks + 1 : blocks + 1 + slabs]
    left_ref, some_ref, own_ref, filter_ref = refs[blocks + 1 + slabs :]
    place = lax.axis_index("ctx")
    length = own_ref.shape[1]
    width = turned[0].shape[1]
    rows = kinds * share
    tokens = blocks * length
    mine = pl.ds(pl.multiple_of(place * length, length), length)
    middle = (place == 1) | (place == 2)
    for m in range(blocks):
        value = grad_refs[m][:, :tokens]
        if m == blocks - 1:
            value = jnp.where(middle, value, grad_refs[blocks][:, :tokens])
        left_ref[m * rows : (m + 1) * rows, :] = value
        for k in range(kinds):
            to = pl.multiple_of(k * share * blocks + (place ^ m) * share, share)
            own_ref[pl.ds(to, share), :] = left_ref[m * rows + k * share : m * rows + (k + 1) * share, mine]
        end = grad_refs[m][:, tokens:].astype(F32)
        cut = end.shape[1]
        size = length - cut
        given = jnp.concatenate([end[:share], end[2 * share :, :size]], axis=1)
        if m == blocks - 1:
            end = grad_refs[blocks][:, tokens:].astype(F32)
            handed = jnp.concatenate([end[share : 2 * share], end[2 * share :, size : 2 * size]], axis=1)
            given = jnp.where(middle, given, handed)
        to = pl.multiple_of((place ^ m) * share, share)
        filter_ref[pl.ds(to, share), :] = given
    for i in range(slabs):
        some_ref[:, i * width : (i + 1) * width] = mm(left_ref[...], turned[i][...]).astype(BF16)


def last_kernel(left_ref, some_ref, turned_ref, first_ref, second_ref):
    half, known = first_ref.shape[0], some_ref.shape[1]
    value = mm(left_ref[...], turned_ref[...]).astype(BF16)
    for i, ref in enumerate((first_ref, second_ref)):
        ref[:, :known] = some_ref[i * half : (i + 1) * half, :]
        ref[:, known:] = value[i * half : (i + 1) * half]


def weight_products(grads, turned, kinds, share):
    blocks, slabs = len(grads) - 1, len(turned)
    tokens, width = turned[0].shape
    rows = kinds * share * blocks
    cost = dict(flops=2 * rows * tokens * width * slabs, bytes_accessed=4 * 2**20, transcendentals=0)
    left, some, own, filters = pl.pallas_call(
        functools.partial(product_kernel, kinds, share, blocks, slabs),
        out_shape=[
            jax.ShapeDtypeStruct((rows, tokens), BF16),
            jax.ShapeDtypeStruct((rows, width * slabs), BF16),
            jax.ShapeDtypeStruct((rows, tokens // blocks), BF16),
            jax.ShapeDtypeStruct((share * blocks, tokens // blocks), F32),
        ],
        in_specs=[VMEM] * (blocks + 1 + slabs),
        out_specs=[VMEM] * 4,
        compiler_params=pltpu.CompilerParams(vmem_limit_bytes=VMEM_BYTES),
        cost_estimate=pl.CostEstimate(**cost),
        name="products",
    )(*grads, *turned)
    return left, some, own, filters


def last_products(left, some, turned):
    rows, known = some.shape
    tokens, width = turned.shape
    half = jax.ShapeDtypeStruct((rows // 2, known + width), BF16)
    return pl.pallas_call(
        last_kernel,
        out_shape=[half, half],
        in_specs=[VMEM] * 3,
        out_specs=[VMEM] * 2,
        compiler_params=pltpu.CompilerParams(vmem_limit_bytes=VMEM_BYTES),
        cost_estimate=pl.CostEstimate(flops=2 * rows * tokens * width, bytes_accessed=2**20, transcendentals=0),
        name="products",
    )(left, some, turned)


def keep_kernel(values_ref, out_ref):
    out_ref[...] = values_ref[...]


def keep(values):
    return pl.pallas_call(
        keep_kernel,
        out_shape=jax.ShapeDtypeStruct(values.shape, values.dtype),
        in_specs=[VMEM],
        out_specs=VMEM,
        compiler_params=pltpu.CompilerParams(vmem_limit_bytes=VMEM_BYTES),
        cost_estimate=pl.CostEstimate(flops=0, bytes_accessed=2**19, transcendentals=0),
        name="keep",
    )(values)


def piece_kernel(values_ref, out_ref):
    width = out_ref.shape[2]
    for i in range(out_ref.shape[0]):
        out_ref[i] = values_ref[:, i * width : (i + 1) * width]


def column_pieces(values, blocks):
    rows, width = values.shape
    return pl.pallas_call(
        piece_kernel,
        out_shape=jax.ShapeDtypeStruct((blocks, rows, width // blocks), values.dtype),
        in_specs=[VMEM],
        out_specs=VMEM,
        compiler_params=pltpu.CompilerParams(vmem_limit_bytes=VMEM_BYTES),
        cost_estimate=pl.CostEstimate(flops=0, bytes_accessed=2**21, transcendentals=0),
        name="pieces",
    )(values)


def input_kernel(count, *refs):
    sums = 0.0
    for grad_ref, weight_ref in zip(refs[:count], refs[count : 2 * count]):
        sums = sums + lax.dot_general(
            grad_ref[...], weight_ref[...], (((0,), (0,)), ((), ())), preferred_element_type=F32
        )
    refs[-1][...] = sums.astype(BF16)


def input_gradient(grads, weights):
    rows, length = grads[0].shape
    width = weights[0].shape[1]
    return pl.pallas_call(
        functools.partial(input_kernel, len(grads)),
        out_shape=jax.ShapeDtypeStruct((length, width), BF16),
        in_specs=[VMEM] * (2 * len(grads)),
        out_specs=VMEM,
        compiler_params=pltpu.CompilerParams(vmem_limit_bytes=VMEM_BYTES),
        cost_estimate=pl.CostEstimate(
            flops=2 * rows * len(grads) * length * width, bytes_accessed=4 * 2**20, transcendentals=0
        ),
        name="inputs",
    )(*grads, *weights)


def place_kernel(kinds, share, factor, *refs):
    out_ref = refs[-1]
    some = (len(refs) - 1) // 2
    blocks = some + 1
    place = lax.axis_index("ctx")
    slab = lax.axis_index("chan") ^ pl.program_id(0)
    width = out_ref.shape[1] // blocks
    source = pl.ds(pl.multiple_of(slab * width, width), width)
    for i, ref in enumerate(refs[:-1]):
        a, r = divmod(i, some)
        sender = lax.rem(place + (r if a else blocks - r), blocks)
        columns = pl.ds(pl.multiple_of(sender * width, width), width)
        for b in range(2):
            for k in range(kinds):
                row = (b * kinds + k) * share
                value = ref[row : row + share, source].astype(F32) * factor
                to = pl.multiple_of(k * share * blocks + (sender ^ (2 * a + b)) * share, share)
                out_ref[pl.ds(to, share), columns] = value


def place_last_kernel(kinds, share, blocks, slabs, factor, *refs):
    out_ref, held, sems = refs[-3:]
    place = lax.axis_index("ctx")
    mine = lax.axis_index("chan")
    width = refs[0].shape[1] // slabs
    copies = []
    for a in range(2):
        sender = lax.rem(place + (blocks - 1 if a else 1), blocks)
        base = (sender ^ (2 * a)) // 2 * 2 * share
        for k in range(kinds):
            for b in range(2):
                row = (b * kinds + k) * share
                to = pl.multiple_of((2 * k + lax.rem(sender + b, 2)) * share, share)
                held[a, pl.ds(to, share), :] = refs[a][row : row + share, :].astype(F32) * factor
            rows = pl.ds(pl.multiple_of(k * share * blocks + base, 2 * share), 2 * share)
            for i in range(slabs):
                columns = pl.ds(pl.multiple_of(((mine ^ i) * blocks + sender) * width, width), width)
                source = held.at[a, 2 * k * share : 2 * (k + 1) * share, i * width : (i + 1) * width]
                copies.append(pltpu.make_async_copy(source, out_ref.at[rows, columns], sems.at[len(copies)]))
                copies[-1].start()
    for copy in copies:
        copy.wait()


def place_weights(pieces, kinds, share, slabs, factor):
    flat = [piece for group in pieces for piece in group[:-1]]
    last = [group[-1] for group in pieces]
    blocks, depth = len(pieces[0]), flat[0].shape[1]
    rows = kinds * share * blocks
    shape = jax.ShapeDtypeStruct((rows, depth * slabs), F32)
    most = pl.pallas_call(
        functools.partial(place_kernel, kinds, share, factor),
        out_shape=shape,
        grid=(slabs,),
        in_specs=[pl.BlockSpec(flat[0].shape, lambda i: (0, 0))] * len(flat),
        out_specs=pl.BlockSpec((rows, depth), lambda i: (0, i)),
        compiler_params=pltpu.CompilerParams(vmem_limit_bytes=VMEM_BYTES),
        cost_estimate=pl.CostEstimate(flops=0, bytes_accessed=6 * 2**20, transcendentals=0),
        name="place",
    )(*flat)
    return pl.pallas_call(
        functools.partial(place_last_kernel, kinds, share, blocks, slabs, factor),
        out_shape=shape,
        in_specs=[VMEM, VMEM, ANY],
        out_specs=ANY,
        scratch_shapes=[
            pltpu.VMEM((2, 2 * kinds * share, depth), F32),
            pltpu.SemaphoreType.DMA((2 * kinds * slabs,)),
        ],
        input_output_aliases={2: 0},
        compiler_params=pltpu.CompilerParams(vmem_limit_bytes=VMEM_BYTES),
        cost_estimate=pl.CostEstimate(flops=0, bytes_accessed=2**20, transcendentals=0),
        name="place",
    )(*last, most)


def swap(values, axis, mask):
    if mask == 0:
        return values
    size = lax.axis_size(axis)
    return lax.ppermute(values, axis, [(i, i ^ mask) for i in range(size)])


def after(values, *others):
    return lax.optimization_barrier((values, *others))[0]


def gather_chan(values):
    slabs = lax.axis_size("chan")
    if slabs != 4:
        return [swap(values, "chan", m) for m in range(slabs)]
    far = swap(values, "chan", 2)
    return [values, swap(values, "chan", 1), far, swap(far, "chan", 1)]


def ring(values, step):
    size = lax.axis_size("ctx")
    found = [values]
    while len(found) < size:
        found.append(lax.ppermute(found[-1], "ctx", [(i, (i + step) % size) for i in range(size)]))
    return found


def general_tail(messages, features, place, mine, kinds, share, factor):
    blocks = lax.axis_size("ctx")
    length, width = features[0].shape
    rows = kinds * share * blocks
    grad_proj = jnp.zeros((kinds, share * blocks, length), BF16)
    grad_filter = jnp.zeros((share * blocks, length), F32)
    for m, message in enumerate(messages):
        piece = lax.dynamic_slice_in_dim(message, (place ^ m) * length, length, 1)
        piece = swap(piece, "ctx", m).reshape(kinds, share, length)
        grad_proj = lax.dynamic_update_slice_in_dim(grad_proj, piece, (place ^ m) * share, 1)
        end = swap(message[:, blocks * length :], "ctx", m).astype(F32)
        end = jnp.concatenate([end[:share], end[2 * share :, : length // 4]], axis=1)
        grad_filter = lax.dynamic_update_slice_in_dim(grad_filter, end, (place ^ m) * share, 0)
    grad_proj = grad_proj.reshape(rows, length)
    grad_weight = jnp.zeros((rows, width * len(features)), F32)
    for m, slab in enumerate(features):
        total = lax.psum(mm(grad_proj, slab).astype(BF16), "ctx").astype(F32) * factor
        grad_weight = lax.dynamic_update_slice_in_dim(grad_weight, total, (mine ^ m) * width, 1)
    return grad_proj, grad_weight, grad_filter


def per_device(activations, proj_weight, long_filter, skip_gain, out_grad):
    blocks = lax.axis_size("ctx")
    slabs = lax.axis_size("chan")
    place = lax.axis_index("ctx")
    mine = lax.axis_index("chan")
    length, width = activations.shape
    kinds, own, depth = proj_weight.shape
    share = own // blocks
    factor = (length * blocks) ** (-0.5)
    rows = kinds * own
    line = blocks == 4 and slabs == 4 and width % (blocks * LANES) == 0 and share % 16 == 0
    weight_rows = proj_weight.reshape(rows, depth)

    def share_of(array, m, axis=0, size=share):
        return lax.dynamic_slice_in_dim(array, (place ^ m) * size, size, axis)

    if line:
        features = [activations, swap(activations, "chan", 1), swap(activations, "chan", 2)]
    else:
        features = [swap(activations, "chan", m) for m in range(slabs)]

    along = [out_grad.astype(F32), long_filter]
    gain = share_of(skip_gain, 0)[None, :]

    weight_cols = [lax.dynamic_slice_in_dim(weight_rows, (mine ^ m) * width, width, 1) for m in range(slabs)]
    if line:
        turned = after(column_pieces(activations, blocks), features[1])
        turned = lax.all_to_all(turned, "ctx", split_axis=0, concat_axis=0).reshape(length * blocks, width // blocks)
        sums = project(weight_rows, [], features[:2], [0, 1])
        weight_cols[1] = swap(weight_cols[1], "chan", 1)
        features[2], sums, along, gain, weight_cols = lax.optimization_barrier(
            (features[2], sums, along, gain, weight_cols)
        )
        features.append(swap(features[2], "chan", 1))
        sums = project(weight_rows, sums, features[2:3], [2])
        pieces = project(weight_rows, sums, features[3:], [3], (blocks, kinds, along))
    else:
        sums = project(weight_rows, [], features[:1], [0])
        pieces = project(weight_rows, sums, features[1:], list(range(1, slabs)), (blocks, kinds, along))
    signals = [swap(piece, "ctx", m) for m, piece in enumerate(pieces)]
    if line:
        signals, turned = lax.optimization_barrier((signals, turned))
        turned = [turned, swap(turned, "chan", 1), swap(turned, "chan", 2)]
    messages = convolve(signals, gain)

    if line:
        messages = [keep(messages[0]), swap(messages[1], "ctx", 1), swap(messages[2], "ctx", 2), messages[3]]
        messages[3] = lax.ppermute(messages[3], "ctx", [(1, 2), (2, 1), (0, 0), (3, 3)])
        messages.append(swap(messages[2], "ctx", 1))
        far, messages = lax.optimization_barrier((turned[2], messages))
        far = swap(far, "chan", 1)
        left, some, grad_proj, grad_filter = weight_products(messages, turned, kinds, share)
        first, second = last_products(left, some, far)
        far_grads = swap(grad_proj, "chan", 2)
        first, second, grad_proj = lax.optimization_barrier((first, second, grad_proj))
        pieces = [ring(first, 1), ring(second, -1)]
        gathered = [grad_proj, swap(grad_proj, "chan", 1)]
        far_grads, gathered[1] = lax.optimization_barrier((far_grads, gathered[1]))
        gathered += [far_grads, swap(far_grads, "chan", 1)]
        weight_cols = after(weight_cols, gathered[2])
        weight_cols = [*weight_cols[:2], swap(weight_cols[2], "chan", 2), swap(weight_cols[3], "chan", 3)]
        grad_rows = input_gradient(gathered, weight_cols)
        grad_rows, pieces[0][-1], pieces[1][-1] = lax.optimization_barrier(
            (grad_rows, pieces[0][-1], pieces[1][-1])
        )
        grad_weight = place_weights(pieces, kinds, share, slabs, factor)
    else:
        grad_proj, grad_weight, grad_filter = general_tail(messages, features, place, mine, kinds, share, factor)
        weight_cols = [swap(cols, "chan", m) for m, cols in enumerate(weight_cols)]
        grad_rows = input_gradient(gather_chan(grad_proj), weight_cols)
    return (
        grad_rows,
        grad_weight.reshape(kinds, own, depth),
        grad_filter,
    )


def solution(mesh):
    placed = (
        P(("files", "ctx"), "chan"),
        P(None, "chan", None),
        P("chan", "ctx"),
        P("chan"),
        P("chan", ("files", "ctx")),
    )
    return jax.shard_map(
        per_device,
        mesh=mesh,
        in_specs=placed,
        out_specs=(
            P(("files", "ctx"), "chan"),
            P("files", "chan", None),
            P("chan", ("files", "ctx")),
        ),
        check_vma=False,
    )
```

```python
import functools
import math

import jax
import jax.numpy as jnp
import numpy as np
from jax import lax
from jax.experimental import pallas as pl
from jax.experimental.pallas import tpu as pltpu
from jax.sharding import PartitionSpec as P

LANES = 128
BF16 = jnp.bfloat16
F32 = jnp.float32
VMEM = pl.BlockSpec(memory_space=pltpu.VMEM)
ANY = pl.BlockSpec(memory_space=pl.ANY)
VMEM_BYTES = 16 * 2**20


def split_table(table):
    high = np.asarray(table, np.float32).astype(BF16)
    low = (np.asarray(table, np.float64) - high.astype(np.float64)).astype(BF16)
    return np.stack([high, low])


def fourier_tables(tokens, group):
    period = 2 * tokens
    rows = period // LANES
    used = rows // 2
    freqs = rows // 2 + 1
    part = -(-freqs * group // 8) * 8
    k1 = np.arange(freqs)
    n1 = np.arange(used)
    angle = 2.0 * math.pi * (np.outer(k1, n1) % rows) / rows
    eye = np.eye(group)
    forward = np.zeros((2 * part, used * group))
    forward[: freqs * group] = np.kron(np.cos(angle), eye)
    forward[part : part + freqs * group] = np.kron(-np.sin(angle), eye)
    weight = np.where((k1 == 0) | (k1 == rows // 2), 1.0, 2.0)[None, :] / period
    inverse = np.zeros((used * group, 2 * part))
    inverse[:, : freqs * group] = np.kron(np.cos(angle.T) * weight, eye)
    inverse[:, part : part + freqs * group] = np.kron(-np.sin(angle.T) * weight, eye)
    n2 = np.arange(LANES)
    turn = 2.0 * math.pi * np.outer(k1, n2) / period
    twiddle = np.zeros((2, part, LANES), np.float32)
    twiddle[0, : freqs * group] = np.repeat(np.cos(turn), group, axis=0)
    twiddle[1, : freqs * group] = np.repeat(np.sin(turn), group, axis=0)
    inner = 2.0 * math.pi * (np.outer(n2, n2) % LANES) / LANES
    cos, sin = np.cos(inner), np.sin(inner)
    second = np.block([[cos, -sin], [sin, cos]])
    second_back = np.block([[cos, sin], [-sin, cos]])
    return (
        split_table(forward),
        split_table(second),
        split_table(second_back),
        split_table(inverse),
        twiddle,
    )


def halves(values):
    high = values.astype(BF16)
    return high, (values - high.astype(F32)).astype(BF16)


def mm(left, right):
    return jnp.dot(left, right, preferred_element_type=F32)


def table_left(table, values):
    high, low = halves(values)
    return mm(table[0], high) + (mm(table[0], low) + mm(table[1], high))


def table_right(values, table):
    high, low = halves(values)
    return mm(high, table[0]) + (mm(low, table[0]) + mm(high, table[1]))


def conv_kernel(blocks, chans, group, factor, *refs):
    count = blocks + 5
    gain_ref, sources, refs = refs[0], refs[1 : 1 + count], refs[1 + count :]
    out_refs = refs[:blocks]
    series, results, inputs = refs[blocks : 3 + blocks]
    held = refs[3 + blocks : 3 + blocks + count]
    sems = refs[3 + blocks + count]
    copies = [pltpu.make_async_copy(sources[i], held[i], sems.at[i]) for i in range(count)]
    for copy in copies:
        copy.start()
    signal_refs = held[:blocks]
    fwd_ref, second_ref, back_ref, inv_ref, twiddle_ref = held[blocks:]
    place = lax.axis_index("ctx")
    length = series.shape[-1]
    cuts = length // LANES
    for m in range(blocks):
        where = place ^ m
        copies[m].wait()
        values = signal_refs[m][...].astype(F32)
        upstream = values[3 * chans : 4 * chans]
        inputs[0, where] = values[:chans]
        inputs[1, where] = values[2 * chans : 3 * chans]
        inputs[2, where] = upstream
        series[0, where] = values[4 * chans :] * factor
        series[1, where] = values[:chans] * values[2 * chans : 3 * chans]
        series[2, where] = upstream * values[chans : 2 * chans]
    for copy in copies[blocks:]:
        copy.wait()
    part = twiddle_ref.shape[1]
    cos, sin = twiddle_ref[0], twiddle_ref[1]
    starts = range(0, chans, group)
    sets = 3 * len(starts)
    picked = []
    for start in starts:
        for q in range(3):
            tiles = []
            for z in range(blocks):
                loaded = series[q, z]
                loaded = loaded[start : start + group]
                for n in range(cuts):
                    tiles.append(loaded[:, n * LANES : (n + 1) * LANES])
            picked.append(jnp.concatenate(tiles, axis=0))
    first = table_left(fwd_ref, jnp.concatenate(picked, axis=1))
    turned = []
    for i in range(sets):
        re = first[:part, i * LANES : (i + 1) * LANES]
        im = first[part:, i * LANES : (i + 1) * LANES]
        turned.append(jnp.concatenate([re * cos + im * sin, im * cos - re * sin], axis=1))
    spectra = table_right(jnp.concatenate(turned, axis=0), second_ref)
    products = []
    for g in range(0, sets, 3):
        (fr, fi), (gr, gi), (ur, ui) = [
            (spectra[i * part : (i + 1) * part, :LANES], spectra[i * part : (i + 1) * part, LANES:])
            for i in range(g, g + 3)
        ]
        products.append(jnp.concatenate([fr * gr - fi * gi, fr * gi + fi * gr], axis=1))
        products.append(jnp.concatenate([fr * ur + fi * ui, fr * ui - fi * ur], axis=1))
        products.append(jnp.concatenate([gr * ur + gi * ui, gr * ui - gi * ur], axis=1))
    back = table_right(jnp.concatenate(products, axis=0), back_ref)
    turned = []
    for i in range(sets):
        re = back[i * part : (i + 1) * part, :LANES]
        im = back[i * part : (i + 1) * part, LANES:]
        turned.append(jnp.concatenate([re * cos - im * sin, im * cos + re * sin], axis=0))
    final = table_left(inv_ref, jnp.concatenate(turned, axis=1))
    for g, start in enumerate(starts):
        for q in range(3):
            at = (3 * g + q) * LANES
            for z in range(blocks):
                tiles = [
                    final[(z * cuts + n) * group : (z * cuts + n + 1) * group, at : at + LANES] for n in range(cuts)
                ]
                results[q, z, start : start + group, :] = jnp.concatenate(tiles, axis=1)
    down = lax.broadcasted_iota(jnp.int32, (chans, chans), 0)
    along = lax.broadcasted_iota(jnp.int32, (chans, chans), 1)
    gain = jnp.sum(jnp.where(down == along, gain_ref[...], 0.0), axis=1, keepdims=True)
    for z in range(blocks):
        conv_out = results[0, z] + gain * series[1, z]
        grad_gated = results[1, z] + gain * series[2, z]
        grads = jnp.concatenate(
            [grad_gated * inputs[1, z], inputs[2, z] * conv_out, grad_gated * inputs[0, z]], axis=0
        ).astype(BF16)
        for ref in out_refs:
            ref[:, z * length : (z + 1) * length] = grads
    found = [(factor * results[2, place ^ m]).astype(BF16).astype(F32) for m in range(blocks)]
    cut = 3 * length // 4
    rest = jnp.zeros((chans, length - cut), F32)
    for m in range(blocks):
        pair = found[m], found[min(m ^ 1, blocks - 1)]
        last = jnp.concatenate([pair[0][:, cut:], pair[1][:, cut:], rest], axis=1)
        rows = jnp.concatenate([pair[0][:, :cut], pair[1][:, :cut], last], axis=0)
        out_refs[m][:, blocks * length :] = rows.astype(BF16)


def convolve(signals, gain):
    blocks = len(signals)
    chans, length = signals[0].shape[0] // 5, signals[0].shape[1]
    tokens = blocks * length
    group = max(1, min(chans, 8, LANES * LANES // tokens))
    tables = fourier_tables(tokens, group)
    arrays = [*signals, *[jnp.asarray(table) for table in tables]]
    part = tables[4].shape[1]
    flops = 2 * 3 * (chans // group) * 3 * (4 * part * group * (tokens // LANES) * LANES + 2 * part * 256 * 256)
    return pl.pallas_call(
        functools.partial(conv_kernel, blocks, chans, group, tokens ** (-0.5)),
        out_shape=[jax.ShapeDtypeStruct((3 * chans, tokens + 3 * length // 4), BF16)] * blocks,
        in_specs=[VMEM] + [ANY] * len(arrays),
        out_specs=[VMEM] * blocks,
        scratch_shapes=[pltpu.VMEM((3, blocks, chans, length), F32)] * 3
        + [pltpu.VMEM(array.shape, array.dtype) for array in arrays]
        + [pltpu.SemaphoreType.DMA((len(arrays),))],
        compiler_params=pltpu.CompilerParams(vmem_limit_bytes=60 * 2**20),
        cost_estimate=pl.CostEstimate(flops=flops, bytes_accessed=4 * 2**20, transcendentals=0),
        name="conv",
    )(gain, *arrays)


def partial_rows(weight_ref, refs, masks):
    mine = lax.axis_index("chan")
    sums = 0.0
    for m, ref in zip(masks, refs):
        width = ref.shape[1]
        at = pl.multiple_of((mine ^ m) * width, width)
        sums = sums + lax.dot_general(
            ref[...], weight_ref[:, pl.ds(at, width)], (((1,), (1,)), ((), ())), preferred_element_type=F32
        )
    return sums


def start_kernel(masks, weight_ref, *refs):
    refs[-1][...] = partial_rows(weight_ref, refs[:-1], masks)


def more_kernel(masks, weight_ref, sum_ref, *refs):
    refs[-1][...] = sum_ref[...] + partial_rows(weight_ref, refs[:-1], masks)


def finish_kernel(masks, blocks, kinds, share, given_ref, filter_ref, weight_ref, sum_ref, *refs):
    out_refs = refs[len(masks) : len(masks) + blocks]
    total = refs[-1]
    place = lax.axis_index("ctx")
    total[...] = (sum_ref[...] + partial_rows(weight_ref, refs[: len(masks)], masks)).T
    for m in range(blocks):
        first = (place ^ m) * share
        rows = [total[pl.ds(pl.multiple_of(k * share * blocks + first, share), share), :] for k in range(kinds)]
        for ref in (given_ref, filter_ref):
            rows.append(ref[pl.ds(pl.multiple_of(first, share), share), :])
        out_refs[m][...] = jnp.concatenate(rows, axis=0).astype(BF16)


def project(weight_rows, sums, features, masks, out=None):
    rows, depth = weight_rows.shape
    length, width = features[0].shape
    along = []
    if out is None:
        body = functools.partial(more_kernel if sums else start_kernel, masks)
        shape = [jax.ShapeDtypeStruct((length, rows), F32)]
    else:
        blocks, kinds, along = out
        share = rows // kinds // blocks
        body = functools.partial(finish_kernel, masks, blocks, kinds, share)
        shape = [jax.ShapeDtypeStruct(((kinds + 2) * share, length), BF16)] * blocks
    flops = 2 * rows * length * width * len(masks)
    return pl.pallas_call(
        body,
        out_shape=shape,
        in_specs=[VMEM] * (len(along) + 1 + len(sums) + len(features)),
        out_specs=[VMEM] * len(shape),
        scratch_shapes=[pltpu.VMEM((rows, length), F32)] if out else [],
        compiler_params=pltpu.CompilerParams(vmem_limit_bytes=VMEM_BYTES),
        cost_estimate=pl.CostEstimate(flops=flops, bytes_accessed=2**20, transcendentals=0),
        name="project",
    )(*along, weight_rows, *sums, *features)


def product_kernel(kinds, share, blocks, slabs, *refs):
    grad_refs, turned = refs[: blocks + 1], refs[blocks + 1 : blocks + 1 + slabs]
    left_ref, some_ref, own_ref, filter_ref = refs[blocks + 1 + slabs :]
    place = lax.axis_index("ctx")
    length = own_ref.shape[1]
    width = turned[0].shape[1]
    rows = kinds * share
    tokens = blocks * length
    mine = pl.ds(pl.multiple_of(place * length, length), length)
    middle = (place == 1) | (place == 2)
    for m in range(blocks):
        value = grad_refs[m][:, :tokens]
        if m == blocks - 1:
            value = jnp.where(middle, value, grad_refs[blocks][:, :tokens])
        left_ref[m * rows : (m + 1) * rows, :] = value
        for k in range(kinds):
            to = pl.multiple_of(k * share * blocks + (place ^ m) * share, share)
            own_ref[pl.ds(to, share), :] = left_ref[m * rows + k * share : m * rows + (k + 1) * share, mine]
        end = grad_refs[m][:, tokens:].astype(F32)
        cut = end.shape[1]
        size = length - cut
        given = jnp.concatenate([end[:share], end[2 * share :, :size]], axis=1)
        if m == blocks - 1:
            end = grad_refs[blocks][:, tokens:].astype(F32)
            handed = jnp.concatenate([end[share : 2 * share], end[2 * share :, size : 2 * size]], axis=1)
            given = jnp.where(middle, given, handed)
        to = pl.multiple_of((place ^ m) * share, share)
        filter_ref[pl.ds(to, share), :] = given
    for i in range(slabs):
        some_ref[:, i * width : (i + 1) * width] = mm(left_ref[...], turned[i][...]).astype(BF16)


def last_kernel(left_ref, some_ref, turned_ref, first_ref, second_ref):
    half, known = first_ref.shape[0], some_ref.shape[1]
    value = mm(left_ref[...], turned_ref[...]).astype(BF16)
    for i, ref in enumerate((first_ref, second_ref)):
        ref[:, :known] = some_ref[i * half : (i + 1) * half, :]
        ref[:, known:] = value[i * half : (i + 1) * half]


def weight_products(grads, turned, kinds, share):
    blocks, slabs = len(grads) - 1, len(turned)
    tokens, width = turned[0].shape
    rows = kinds * share * blocks
    cost = dict(flops=2 * rows * tokens * width * slabs, bytes_accessed=4 * 2**20, transcendentals=0)
    left, some, own, filters = pl.pallas_call(
        functools.partial(product_kernel, kinds, share, blocks, slabs),
        out_shape=[
            jax.ShapeDtypeStruct((rows, tokens), BF16),
            jax.ShapeDtypeStruct((rows, width * slabs), BF16),
            jax.ShapeDtypeStruct((rows, tokens // blocks), BF16),
            jax.ShapeDtypeStruct((share * blocks, tokens // blocks), F32),
        ],
        in_specs=[VMEM] * (blocks + 1 + slabs),
        out_specs=[VMEM] * 4,
        compiler_params=pltpu.CompilerParams(vmem_limit_bytes=VMEM_BYTES),
        cost_estimate=pl.CostEstimate(**cost),
        name="products",
    )(*grads, *turned)
    return left, some, own, filters


def last_products(left, some, turned):
    rows, known = some.shape
    tokens, width = turned.shape
    half = jax.ShapeDtypeStruct((rows // 2, known + width), BF16)
    return pl.pallas_call(
        last_kernel,
        out_shape=[half, half],
        in_specs=[VMEM] * 3,
        out_specs=[VMEM] * 2,
        compiler_params=pltpu.CompilerParams(vmem_limit_bytes=VMEM_BYTES),
        cost_estimate=pl.CostEstimate(flops=2 * rows * tokens * width, bytes_accessed=2**20, transcendentals=0),
        name="products",
    )(left, some, turned)


def keep_kernel(values_ref, out_ref):
    out_ref[...] = values_ref[...]


def keep(values):
    return pl.pallas_call(
        keep_kernel,
        out_shape=jax.ShapeDtypeStruct(values.shape, values.dtype),
        in_specs=[VMEM],
        out_specs=VMEM,
        compiler_params=pltpu.CompilerParams(vmem_limit_bytes=VMEM_BYTES),
        cost_estimate=pl.CostEstimate(flops=0, bytes_accessed=2**19, transcendentals=0),
        name="keep",
    )(values)


def piece_kernel(values_ref, out_ref):
    width = out_ref.shape[2]
    for i in range(out_ref.shape[0]):
        out_ref[i] = values_ref[:, i * width : (i + 1) * width]


def column_pieces(values, blocks):
    rows, width = values.shape
    return pl.pallas_call(
        piece_kernel,
        out_shape=jax.ShapeDtypeStruct((blocks, rows, width // blocks), values.dtype),
        in_specs=[VMEM],
        out_specs=VMEM,
        compiler_params=pltpu.CompilerParams(vmem_limit_bytes=VMEM_BYTES),
        cost_estimate=pl.CostEstimate(flops=0, bytes_accessed=2**21, transcendentals=0),
        name="pieces",
    )(values)


def input_kernel(count, *refs):
    sums = 0.0
    for grad_ref, weight_ref in zip(refs[:count], refs[count : 2 * count]):
        sums = sums + lax.dot_general(
            grad_ref[...], weight_ref[...], (((0,), (0,)), ((), ())), preferred_element_type=F32
        )
    refs[-1][...] = sums.astype(BF16)


def input_gradient(grads, weights):
    rows, length = grads[0].shape
    width = weights[0].shape[1]
    return pl.pallas_call(
        functools.partial(input_kernel, len(grads)),
        out_shape=jax.ShapeDtypeStruct((length, width), BF16),
        in_specs=[VMEM] * (2 * len(grads)),
        out_specs=VMEM,
        compiler_params=pltpu.CompilerParams(vmem_limit_bytes=VMEM_BYTES),
        cost_estimate=pl.CostEstimate(
            flops=2 * rows * len(grads) * length * width, bytes_accessed=4 * 2**20, transcendentals=0
        ),
        name="inputs",
    )(*grads, *weights)


def place_kernel(kinds, share, factor, *refs):
    out_ref = refs[-1]
    some = (len(refs) - 1) // 2
    blocks = some + 1
    place = lax.axis_index("ctx")
    slab = lax.axis_index("chan") ^ pl.program_id(0)
    width = out_ref.shape[1] // blocks
    source = pl.ds(pl.multiple_of(slab * width, width), width)
    for i, ref in enumerate(refs[:-1]):
        a, r = divmod(i, some)
        sender = lax.rem(place + (r if a else blocks - r), blocks)
        columns = pl.ds(pl.multiple_of(sender * width, width), width)
        for b in range(2):
            for k in range(kinds):
                row = (b * kinds + k) * share
                value = ref[row : row + share, source].astype(F32) * factor
                to = pl.multiple_of(k * share * blocks + (sender ^ (2 * a + b)) * share, share)
                out_ref[pl.ds(to, share), columns] = value


def place_last_kernel(kinds, share, blocks, slabs, factor, *refs):
    out_ref, held, sems = refs[-3:]
    place = lax.axis_index("ctx")
    mine = lax.axis_index("chan")
    width = refs[0].shape[1] // slabs
    copies = []
    for a in range(2):
        sender = lax.rem(place + (blocks - 1 if a else 1), blocks)
        base = (sender ^ (2 * a)) // 2 * 2 * share
        for k in range(kinds):
            for b in range(2):
                row = (b * kinds + k) * share
                to = pl.multiple_of((2 * k + lax.rem(sender + b, 2)) * share, share)
                held[a, pl.ds(to, share), :] = refs[a][row : row + share, :].astype(F32) * factor
            rows = pl.ds(pl.multiple_of(k * share * blocks + base, 2 * share), 2 * share)
            for i in range(slabs):
                columns = pl.ds(pl.multiple_of(((mine ^ i) * blocks + sender) * width, width), width)
                source = held.at[a, 2 * k * share : 2 * (k + 1) * share, i * width : (i + 1) * width]
                copies.append(pltpu.make_async_copy(source, out_ref.at[rows, columns], sems.at[len(copies)]))
                copies[-1].start()
    for copy in copies:
        copy.wait()


def place_weights(pieces, kinds, share, slabs, factor):
    flat = [piece for group in pieces for piece in group[:-1]]
    last = [group[-1] for group in pieces]
    blocks, depth = len(pieces[0]), flat[0].shape[1]
    rows = kinds * share * blocks
    shape = jax.ShapeDtypeStruct((rows, depth * slabs), F32)
    most = pl.pallas_call(
        functools.partial(place_kernel, kinds, share, factor),
        out_shape=shape,
        grid=(slabs,),
        in_specs=[pl.BlockSpec(flat[0].shape, lambda i: (0, 0))] * len(flat),
        out_specs=pl.BlockSpec((rows, depth), lambda i: (0, i)),
        compiler_params=pltpu.CompilerParams(vmem_limit_bytes=VMEM_BYTES),
        cost_estimate=pl.CostEstimate(flops=0, bytes_accessed=6 * 2**20, transcendentals=0),
        name="place",
    )(*flat)
    return pl.pallas_call(
        functools.partial(place_last_kernel, kinds, share, blocks, slabs, factor),
        out_shape=shape,
        in_specs=[VMEM, VMEM, ANY],
        out_specs=ANY,
        scratch_shapes=[
            pltpu.VMEM((2, 2 * kinds * share, depth), F32),
            pltpu.SemaphoreType.DMA((2 * kinds * slabs,)),
        ],
        input_output_aliases={2: 0},
        compiler_params=pltpu.CompilerParams(vmem_limit_bytes=VMEM_BYTES),
        cost_estimate=pl.CostEstimate(flops=0, bytes_accessed=2**20, transcendentals=0),
        name="place",
    )(*last, most)


def swap(values, axis, mask):
    if mask == 0:
        return values
    size = lax.axis_size(axis)
    return lax.ppermute(values, axis, [(i, i ^ mask) for i in range(size)])


def after(values, *others):
    return lax.optimization_barrier((values, *others))[0]


def gather_chan(values):
    slabs = lax.axis_size("chan")
    if slabs != 4:
        return [swap(values, "chan", m) for m in range(slabs)]
    far = swap(values, "chan", 2)
    return [values, swap(values, "chan", 1), far, swap(far, "chan", 1)]


def ring(values, step):
    size = lax.axis_size("ctx")
    found = [values]
    while len(found) < size:
        found.append(lax.ppermute(found[-1], "ctx", [(i, (i + step) % size) for i in range(size)]))
    return found


def general_tail(messages, features, place, mine, kinds, share, factor):
    blocks = lax.axis_size("ctx")
    length, width = features[0].shape
    rows = kinds * share * blocks
    grad_proj = jnp.zeros((kinds, share * blocks, length), BF16)
    grad_filter = jnp.zeros((share * blocks, length), F32)
    for m, message in enumerate(messages):
        piece = lax.dynamic_slice_in_dim(message, (place ^ m) * length, length, 1)
        piece = swap(piece, "ctx", m).reshape(kinds, share, length)
        grad_proj = lax.dynamic_update_slice_in_dim(grad_proj, piece, (place ^ m) * share, 1)
        end = swap(message[:, blocks * length :], "ctx", m).astype(F32)
        end = jnp.concatenate([end[:share], end[2 * share :, : length // 4]], axis=1)
        grad_filter = lax.dynamic_update_slice_in_dim(grad_filter, end, (place ^ m) * share, 0)
    grad_proj = grad_proj.reshape(rows, length)
    grad_weight = jnp.zeros((rows, width * len(features)), F32)
    for m, slab in enumerate(features):
        total = lax.psum(mm(grad_proj, slab).astype(BF16), "ctx").astype(F32) * factor
        grad_weight = lax.dynamic_update_slice_in_dim(grad_weight, total, (mine ^ m) * width, 1)
    return grad_proj, grad_weight, grad_filter


def per_device(activations, proj_weight, long_filter, skip_gain, out_grad):
    blocks = lax.axis_size("ctx")
    slabs = lax.axis_size("chan")
    place = lax.axis_index("ctx")
    mine = lax.axis_index("chan")
    length, width = activations.shape
    kinds, own, depth = proj_weight.shape
    share = own // blocks
    factor = (length * blocks) ** (-0.5)
    rows = kinds * own
    line = blocks == 4 and slabs == 4 and width % (blocks * LANES) == 0 and share % 16 == 0
    weight_rows = proj_weight.reshape(rows, depth)

    def share_of(array, m, axis=0, size=share):
        return lax.dynamic_slice_in_dim(array, (place ^ m) * size, size, axis)

    if line:
        features = [activations, swap(activations, "chan", 1), swap(activations, "chan", 2)]
    else:
        features = [swap(activations, "chan", m) for m in range(slabs)]

    along = [out_grad.astype(F32), long_filter]
    gain = share_of(skip_gain, 0)[None, :]

    weight_cols = [lax.dynamic_slice_in_dim(weight_rows, (mine ^ m) * width, width, 1) for m in range(slabs)]
    if line:
        turned = after(column_pieces(activations, blocks), features[1])
        turned = lax.all_to_all(turned, "ctx", split_axis=0, concat_axis=0).reshape(length * blocks, width // blocks)
        sums = project(weight_rows, [], features[:2], [0, 1])
        weight_cols[1] = swap(weight_cols[1], "chan", 1)
        features[2], sums, along, gain, weight_cols = lax.optimization_barrier(
            (features[2], sums, along, gain, weight_cols)
        )
        features.append(swap(features[2], "chan", 1))
        sums = project(weight_rows, sums, features[2:3], [2])
        pieces = project(weight_rows, sums, features[3:], [3], (blocks, kinds, along))
    else:
        sums = project(weight_rows, [], features[:1], [0])
        pieces = project(weight_rows, sums, features[1:], list(range(1, slabs)), (blocks, kinds, along))
    signals = [swap(piece, "ctx", m) for m, piece in enumerate(pieces)]
    if line:
        signals, turned = lax.optimization_barrier((signals, turned))
        turned = [turned, swap(turned, "chan", 1), swap(turned, "chan", 2)]
    messages = convolve(signals, gain)

    if line:
        messages = [keep(messages[0]), swap(messages[1], "ctx", 1), swap(messages[2], "ctx", 2), messages[3]]
        messages[3] = lax.ppermute(messages[3], "ctx", [(1, 2), (2, 1), (0, 0), (3, 3)])
        messages.append(swap(messages[2], "ctx", 1))
        far, messages = lax.optimization_barrier((turned[2], messages))
        far = swap(far, "chan", 1)
        left, some, grad_proj, grad_filter = weight_products(messages, turned, kinds, share)
        first, second = last_products(left, some, far)
        far_grads = swap(grad_proj, "chan", 2)
        first, second, grad_proj = lax.optimization_barrier((first, second, grad_proj))
        pieces = [ring(first, 1), ring(second, -1)]
        gathered = [grad_proj, swap(grad_proj, "chan", 1)]
        far_grads, gathered[1] = lax.optimization_barrier((far_grads, gathered[1]))
        gathered += [far_grads, swap(far_grads, "chan", 1)]
        weight_cols = after(weight_cols, gathered[2])
        weight_cols = [*weight_cols[:2], swap(weight_cols[2], "chan", 2), swap(weight_cols[3], "chan", 3)]
        grad_rows = input_gradient(gathered, weight_cols)
        grad_rows, pieces[0][-1], pieces[1][-1] = lax.optimization_barrier(
            (grad_rows, pieces[0][-1], pieces[1][-1])
        )
        grad_weight = place_weights(pieces, kinds, share, slabs, factor)
    else:
        grad_proj, grad_weight, grad_filter = general_tail(messages, features, place, mine, kinds, share, factor)
        weight_cols = [swap(cols, "chan", m) for m, cols in enumerate(weight_cols)]
        grad_rows = input_gradient(gather_chan(grad_proj), weight_cols)
    return (
        grad_rows,
        grad_weight.reshape(kinds, own, depth),
        grad_filter,
    )


def solution(mesh):
    placed = (
        P(("files", "ctx"), "chan"),
        P(None, "chan", None),
        P("chan", "ctx"),
        P("chan"),
        P("chan", ("files", "ctx")),
    )
    return jax.shard_map(
        per_device,
        mesh=mesh,
        in_specs=placed,
        out_specs=(
            P(("files", "ctx"), "chan"),
            P("files", "chan", None),
            P("chan", ("files", "ctx")),
        ),
        check_vma=False,
    )
```
